256 devices in a mesh: grp: 8 (over z_lo, core), dev: 32 (over y, z_hi, x).
Axes of the slice: x: 4, y: 4, z: 8 (z_hi: 2, z_lo: 4; z = z_hi * 4 + z_lo), core: 2. Of those that a mesh axis runs over, the one named last changes fastest.
Arguments:
- q_embed: bfloat16 [32768, 1024], P(('grp', 'dev')), may hold values from -16 to 16
- p_embed: bfloat16 [32768, 1024], P(('grp', 'dev')), may hold values from -16 to 16
- positives: int32 [32768], P(('grp', 'dev')), may hold values from 0 to 4095, as said below
Outputs:
- mean_loss: float32 [], replicated
- grad_query: float32 [32768, 1024], P(('grp', 'dev'))
- grad_passage: float32 [32768, 1024], P(('grp', 'dev'))
The draws below stay inside these ranges and needn't reach their ends.
Inputs may be any that keep to these rules, and one draw needn't show every extreme that they name: `positives`: within each group of 4096 consecutive queries every passage index appears exactly once.
All inputs are finite; a program needn't handle non-finite values.
Results may differ from the reference program's by a relative error of at most 0.0057.
Values may be sent and summed in bfloat16 or wider, within the bound.
No kernel may reach another device: no remote copies, remote signals or barrier semaphores. Data moves between devices by JAX's collectives and lax.ppermute only.
A program may use at most 64 MiB of HBM per device.

```python
import jax
import jax.numpy as jnp
from jax import lax

D = 1024
GR = 4096
TOKENS = 32768


def positive_order(key):
    groups = TOKENS // GR
    group_keys = jax.random.split(jax.random.fold_in(key, 7), groups)
    orders = jax.vmap(lambda sub_key: jax.random.permutation(sub_key, GR))(group_keys)
    return orders.reshape(TOKENS).astype(jnp.int32)


def query_rows(key, twin_share, scale_low, scale_high):
    key = jax.random.fold_in(key, 13)
    dir_key, mark_key, scale_key = jax.random.split(key, 3)
    directions = jnp.clip(jax.random.normal(dir_key, (TOKENS, D), jnp.float32), -5.0, 5.0)
    marked = jax.random.uniform(mark_key, (TOKENS, 1), jnp.float32) < twin_share
    twins = jnp.roll(directions, 1, axis=0) + 0.15 * directions
    directions = jnp.where(marked, twins, directions)
    scales = jnp.exp(jax.random.uniform(scale_key, (TOKENS, 1), jnp.float32, jnp.log(scale_low), jnp.log(scale_high)))
    return (directions, scales)


def draw_positives(key, part):
    return positive_order(key)


def draw_q_embed(key, part):
    directions, scales = query_rows(key, 0.0, 1.0, 4.0)
    return jnp.clip(directions * scales, -16.0, 16.0).astype(jnp.bfloat16)


def draw_p_embed(key, part):
    directions, scales = query_rows(key, 0.0, 1.0, 4.0)
    scale_low, scale_high = (1.0, 4.0)
    order = positive_order(key)
    key = jax.random.fold_in(key, 5)
    noise_key, strength_key, scale_key = jax.random.split(key, 3)
    noise = jnp.clip(jax.random.normal(noise_key, (TOKENS, D), jnp.float32), -5.0, 5.0)
    strength = jnp.exp(jax.random.uniform(strength_key, (TOKENS, 1), jnp.float32, jnp.log(0.08), jnp.log(4.0)))
    rows = (strength * directions + noise) / jnp.sqrt(strength * strength + 1.0)
    row_scales = jnp.exp(jax.random.uniform(scale_key, (TOKENS, 1), jnp.float32, jnp.log(scale_low), jnp.log(scale_high)))
    rows = jnp.clip(rows * row_scales, -16.0, 16.0)
    target = jnp.arange(TOKENS, dtype=jnp.int32) // GR * GR + order
    passages = jnp.zeros((TOKENS, D), jnp.float32).at[target].set(rows)
    return passages.astype(jnp.bfloat16)


def setup_inputs(seed: int = 0) -> dict:
    seeds = jax.random.split(jax.random.key(seed), 4)
    return {
        "q_embed": draw_q_embed(jax.random.fold_in(seeds[3], 71), 0),
        "p_embed": draw_p_embed(jax.random.fold_in(seeds[3], 71), 0),
        "positives": draw_positives(jax.random.fold_in(seeds[3], 71), 0),
    }


INV_TEMP = 100.0

def normalize(values):
    return values * lax.rsqrt(lax.optimization_barrier(jnp.sum(values * values, axis=-1, keepdims=True)) + 1e-06)

def log_total(scores, axis):
    top = lax.optimization_barrier(jnp.max(scores, axis=axis, keepdims=True))
    return jnp.squeeze(top, axis) + jnp.log(lax.optimization_barrier(jnp.sum(jnp.exp(scores - top), axis=axis)))

def group_terms(pieces):
    query_raw, passage_raw, index_pos = pieces
    query_float = query_raw.astype(jnp.float32)
    passage_float = passage_raw.astype(jnp.float32)
    query_unit = normalize(query_float).astype(jnp.bfloat16)
    passage_unit = normalize(passage_float).astype(jnp.bfloat16)
    width = query_unit.shape[0]
    ident = jnp.arange(width)
    diagonal = ident[:, None] == ident[None, :]
    score_qp = jnp.dot(query_unit, passage_unit.T, preferred_element_type=jnp.float32) * INV_TEMP
    score_qq = jnp.dot(query_unit, query_unit.T, preferred_element_type=jnp.float32) * INV_TEMP
    score_pp = jnp.dot(passage_unit, passage_unit.T, preferred_element_type=jnp.float32) * INV_TEMP
    score_qq = jnp.where(diagonal, -jnp.inf, score_qq)
    score_pp = jnp.where(diagonal, -jnp.inf, score_pp)
    log_b = jnp.logaddexp(log_total(score_qp, 1), log_total(score_qq, 1))
    log_a = jnp.logaddexp(log_total(score_qp, 0), log_total(score_pp, 1))
    lzq = jnp.logaddexp(log_b, log_a[index_pos])
    positive_score = lax.optimization_barrier(jnp.sum(jnp.where(index_pos[:, None] == ident[None, :], score_qp, 0.0), axis=1))
    loss_sum = jnp.sum(lzq - positive_score)
    lzp = jnp.zeros_like(lzq).at[index_pos].set(lzq)
    hit = (index_pos[:, None] == ident[None, :]).astype(jnp.float32)
    g_qp = (jnp.exp(score_qp - lzq[:, None]) + jnp.exp(score_qp - lzp[None, :]) - hit).astype(jnp.bfloat16)
    g_qq = (jnp.exp(score_qq - lzq[:, None]) + jnp.exp(score_qq - lzq[None, :])).astype(jnp.bfloat16)
    g_pp = (jnp.exp(score_pp - lzp[:, None]) + jnp.exp(score_pp - lzp[None, :])).astype(jnp.bfloat16)
    grad_qunit = INV_TEMP * (jnp.dot(g_qp, passage_unit, preferred_element_type=jnp.float32) + jnp.dot(g_qq, query_unit, preferred_element_type=jnp.float32))
    grad_punit = INV_TEMP * (jnp.dot(g_qp.T, query_unit, preferred_element_type=jnp.float32) + jnp.dot(g_pp, passage_unit, preferred_element_type=jnp.float32))
    _, pull_query = jax.vjp(normalize, query_float)
    _, pull_passage = jax.vjp(normalize, passage_float)
    return (loss_sum, pull_query(grad_qunit)[0], pull_passage(grad_punit)[0])

def reference(q_embed, p_embed, positives):
    groups = TOKENS // GR
    loss_sums, grad_q, grad_p = lax.map(group_terms, (q_embed.reshape(groups, GR, D), p_embed.reshape(groups, GR, D), positives.reshape(groups, GR)))
    mean_loss = jnp.sum(loss_sums) / TOKENS
    return (mean_loss, grad_q.reshape(TOKENS, D), grad_p.reshape(TOKENS, D))
```

```python
import functools

import jax
import jax.numpy as jnp
from jax import lax
from jax.experimental import pallas as pl
from jax.experimental.pallas import tpu as pltpu
from jax.sharding import PartitionSpec as P

INV_TEMP = 100.0
EPS = 1e-06
NY, NZ, NX = 4, 2, 4
ROWS = 128
SHARD = 2 * ROWS
PAD = 16
WIDTH = 1024
MASKED = -1e30
F32 = jnp.float32
BF16 = jnp.bfloat16
VMEM = pl.BlockSpec(memory_space=pltpu.VMEM)
SMEM = pl.BlockSpec(memory_space=pltpu.SMEM)
NT = (((1,), (1,)), ((), ()))


def dev_index(y, z, x):
    return (y % NY) * (NZ * NX) + (z % NZ) * NX + x % NX


def shift(value, dy, dz, dx):
    pairs = [
        (dev_index(y, z, x), dev_index(y + dy, z + dz, x + dx))
        for y in range(NY)
        for z in range(NZ)
        for x in range(NX)
    ]
    return lax.ppermute(value, "dev", pairs)


def params(mib):
    return pltpu.CompilerParams(vmem_limit_bytes=mib * 1024 * 1024)


def lse2(left, right):
    top = jnp.maximum(left, right)
    return top + jnp.log(jnp.exp(left - top) + jnp.exp(right - top))


def iota(shape, dim):
    return lax.broadcasted_iota(jnp.int32, shape, dim)


def to_row(column):
    eye = iota((ROWS, ROWS), 0) == iota((ROWS, ROWS), 1)
    return jnp.sum(jnp.where(eye, column, 0.0), axis=0, keepdims=True)


def to_column(row):
    eye = iota((ROWS, ROWS), 0) == iota((ROWS, ROWS), 1)
    return jnp.sum(jnp.where(eye, row, 0.0), axis=1, keepdims=True)


def norm_kernel(pos_ref, q_ref, p_ref, out_ref):
    for part, ref in enumerate((q_ref, p_ref)):
        values = ref[...].astype(F32)
        scale = lax.rsqrt(jnp.sum(values * values, axis=1, keepdims=True) + EPS)
        out_ref[part * ROWS : (part + 1) * ROWS, :] = (values * scale).astype(BF16)
    pos = pos_ref[...]
    high = jnp.broadcast_to((pos >> 6).astype(F32), (PAD, ROWS))
    low = jnp.broadcast_to((pos & 63).astype(F32), (PAD, ROWS))
    out_ref[SHARD:, 0:ROWS] = high.astype(BF16)
    out_ref[SHARD:, ROWS : 2 * ROWS] = low.astype(BF16)
    out_ref[SHARD:, 2 * ROWS :] = jnp.zeros((PAD, WIDTH - 2 * ROWS), BF16)


def fwd_kernel(first, *refs):
    if first:
        coord, *refs = refs
    else:
        coord, pos_ref, before, *refs = refs
    rows, cols = refs[:NX], refs[NX : NX + NY]
    score_ref, stat_ref, row_scr = refs[NX + NY :]
    y, z, x = coord[0], coord[1], coord[2]
    for k in range(NX):
        row_scr[k * SHARD : (k + 1) * SHARD, :] = rows[k][0:SHARD, :]
    for j in range(NY):

        @pl.loop(0, NX)
        def _(k):
            at = pl.ds(pl.multiple_of(k * SHARD, SHARD), SHARD)
            block = lax.dot_general(
                row_scr[at, :], cols[j][0:SHARD, :], NT, preferred_element_type=F32
            )
            score_ref[at, j * SHARD : (j + 1) * SHARD] = block * INV_TEMP

    if first:
        diagonal = iota((SHARD, SHARD), 0) == iota((SHARD, SHARD), 1)
        score_ref[0:SHARD, 0:SHARD] = jnp.where(diagonal, MASKED, score_ref[0:SHARD, 0:SHARD])

    hits = jnp.zeros((ROWS, ROWS), F32)
    for j in range(NY):
        high = cols[j][SHARD : SHARD + PAD, 0:ROWS].astype(F32)[0:1, :]
        low = cols[j][SHARD : SHARD + PAD, ROWS : 2 * ROWS].astype(F32)[0:1, :]
        pos = (high * 64.0 + low).astype(jnp.int32)
        owner = pos >> 7
        here = ((owner >> 3) == y) & (((owner >> 2) & 1) == z)
        slot = (x - (owner & 3)) & 3
        row_id = jnp.where(here, slot * ROWS + (pos & 127), -1)
        for k in range(NX):
            block = score_ref[
                k * SHARD + ROWS : (k + 1) * SHARD, j * SHARD : j * SHARD + ROWS
            ]
            hit = (iota((ROWS, ROWS), 0) + k * ROWS) == row_id
            hits = hits + jnp.where(hit, block, 0.0)
    hit_row = jnp.sum(hits, axis=0, keepdims=True)

    stat_ref[...] = jnp.zeros_like(stat_ref)

    @pl.loop(0, NX)
    def _(k):
        for part in range(2):
            at = pl.ds(pl.multiple_of(k * SHARD + part * ROWS, ROWS), ROWS)
            block = score_ref[at, :]
            top = jnp.max(block, axis=1, keepdims=True)
            total = jnp.sum(jnp.exp(block - top), axis=1, keepdims=True)
            stat_ref[pl.ds(part * NX + k, 1), :] = to_row(top + jnp.log(total))

    if first:
        stat_ref[8:9, :] = hit_row
    else:
        stat_ref[0:8, :] = lse2(stat_ref[0:8, :], before[0:8, :])
        stat_ref[8:9, :] = hit_row + before[8:9, :]
        stat_ref[9:10, :] = pos_ref[...].astype(F32)


def join_x_kernel(coord, s0, s1, s2, s3, out_ref, scr, hit_scr):
    x = coord[2]
    stats = (s0, s1, s2, s3)
    for d in range(NX):
        at = (x - d) & 3
        for part in range(2):
            for k in range(NX):
                scr[at, part * NX + k : part * NX + k + 1, :] = stats[d][
                    part * NX + (k - d) % NX : part * NX + (k - d) % NX + 1, :
                ]
        hit_scr[at, 0:1, :] = stats[d][8:9, :]
        out_ref[8 + d : 9 + d, :] = stats[d][9:10, :]
    top = jnp.maximum(jnp.maximum(scr[0], scr[1]), jnp.maximum(scr[2], scr[3]))
    total = jnp.exp(scr[0] - top) + jnp.exp(scr[1] - top)
    total = total + jnp.exp(scr[2] - top) + jnp.exp(scr[3] - top)
    out_ref[0:8, :] = top + jnp.log(total)
    hit = hit_scr[0, 0:1, :] + hit_scr[1, 0:1, :] + hit_scr[2, 0:1, :] + hit_scr[3, 0:1, :]
    out_ref[12:13, :] = hit
    out_ref[13:16, :] = jnp.zeros((3, ROWS), F32)


def mid_kernel(coord, c0, c1, c2, c3, rows_ref, cols_ref, ids_ref, loss_ref, sum_scr):
    y, z, x = coord[0], coord[1], coord[2]
    parts = (c0, c1, c2, c3)
    count = NY * NZ * NX

    def table(first_row):
        return jnp.concatenate(
            [
                parts[jy][jz * 16 + first_row : jz * 16 + first_row + NX, :]
                for jy in range(NY)
                for jz in range(NZ)
            ],
            axis=0,
        )

    log_b, log_a, pos = table(0), table(4), table(8).astype(jnp.int32)
    owner = pos >> 7
    lane = pos & 127
    jy = (y - (owner >> 3)) & 3
    jz = ((owner >> 2) & 1) ^ z
    slot = (jy * NZ + jz) * NX + ((x - (owner & 3)) & 3)
    log_a_pos = jnp.zeros((count, ROWS), F32)
    for r in range(count):
        picked = jnp.take_along_axis(
            jnp.broadcast_to(log_a[r : r + 1, :], (count, ROWS)), lane, axis=1
        )
        log_a_pos = jnp.where(slot == r, picked, log_a_pos)
    lzq = lse2(log_b, log_a_pos)

    part_high = lzq.astype(BF16).astype(F32)
    part_mid = (lzq - part_high).astype(BF16).astype(F32)
    part_low = lzq - part_high - part_mid
    lane_row = iota((1, ROWS), 1).astype(F32)
    total = jnp.zeros((5 * count, ROWS), F32)
    for group in range(0, count, 2):
        left, right = [], []
        for r in (group, group + 1):
            chosen = iota((count, ROWS), 0) == slot[r : r + 1, :]
            values = (
                part_high[r : r + 1, :],
                part_mid[r : r + 1, :],
                part_low[r : r + 1, :],
                jnp.full((1, ROWS), float(r), F32),
                lane_row,
            )
            left.append(
                jnp.concatenate([jnp.where(chosen, v, 0.0) for v in values], axis=0).astype(BF16)
            )
            right.append((iota((ROWS, ROWS), 0) == lane[r : r + 1, :]).astype(F32).astype(BF16))
        total = total + lax.dot_general(
            jnp.concatenate(left, axis=1),
            jnp.concatenate(right, axis=1),
            NT,
            preferred_element_type=F32,
        )
    lzp = (total[0:count] + total[count : 2 * count]) + total[2 * count : 3 * count]
    from_slot = total[3 * count : 4 * count].astype(jnp.int32)
    from_lane = total[4 * count :].astype(jnp.int32)
    id_q = slot * SHARD + ROWS + lane
    id_p = from_slot * SHARD + from_lane

    rows_ref[0:NX, :] = lzq[0:NX, :]
    rows_ref[NX : 2 * NX, :] = lzp[0:NX, :]
    for jz_ in range(NZ):
        for jy_ in range(NY):
            r = (jy_ * NZ + jz_) * NX
            at = (jz_ * NY + jy_) * SHARD
            cols_ref[0:1, at : at + ROWS] = lzq[r : r + 1, :]
            cols_ref[0:1, at + ROWS : at + SHARD] = lzp[r : r + 1, :]
            ids_ref[0:1, at : at + ROWS] = id_q[r : r + 1, :]
            ids_ref[0:1, at + ROWS : at + SHARD] = id_p[r : r + 1, :]

    for jy_ in range(NY):
        for jz_ in range(NZ):
            lead = ((y - jy_) & 3) * NZ + (z ^ jz_)
            for kx in range(NX):
                r = (jy_ * NZ + jz_) * NX + kx
                sum_scr[lead * NX + ((x - kx) & 3), 0:1, :] = lzq[r : r + 1, :]
            sum_scr[count + lead, 0:1, :] = -parts[jy_][jz_ * 16 + 12 : jz_ * 16 + 13, :]
    row = sum_scr[0, 0:1, :]
    for r in range(1, count + NY * NZ):
        row = row + sum_scr[r, 0:1, :]
    loss_ref[...] = jnp.broadcast_to(jnp.sum(row, axis=1, keepdims=True), (1, ROWS))


def bwd_kernel(slots, rows_ref, cols_ref, ids_ref, s0_ref, s1_ref, *refs):
    cols = refs[: NY * NZ]
    outs = refs[NY * NZ : NY * NZ + len(slots)]
    g_scr, col_scr = refs[NY * NZ + len(slots) :]
    for j, ref in enumerate(cols):
        col_scr[j * SHARD : (j + 1) * SHARD, :] = ref[0:SHARD, :]
    for k, out_ref in zip(slots, outs):
        for part in range(2):
            own = to_column(rows_ref[part * NX + k : part * NX + k + 1, :])
            first = k * SHARD + part * ROWS
            for half, score_ref in enumerate((s0_ref, s1_ref)):

                @pl.loop(0, NY * 2)
                def _(j):
                    at = pl.ds(pl.multiple_of(j * ROWS, ROWS), ROWS)
                    there = pl.ds(pl.multiple_of(half * NY * SHARD + j * ROWS, ROWS), ROWS)
                    block = score_ref[first : first + ROWS, at]
                    hit = (iota((ROWS, ROWS), 0) + first) == ids_ref[0:1, there]
                    grad = jnp.exp(block - own) + jnp.exp(block - cols_ref[0:1, there])
                    grad = grad - jnp.where(hit, 1.0, 0.0)
                    g_scr[part * ROWS : (part + 1) * ROWS, there] = grad.astype(BF16)

        @pl.loop(0, WIDTH // 256)
        def _(n):
            at = pl.ds(pl.multiple_of(n * 256, 256), 256)
            partial = jnp.dot(g_scr[...], col_scr[:, at], preferred_element_type=F32)
            out_ref[:, at] = (partial * INV_TEMP).astype(out_ref.dtype)


def final_kernel(own, r1, r2, r3, q_ref, p_ref, gq_ref, gp_ref):
    for part, (raw, out_ref) in enumerate(((q_ref, gq_ref), (p_ref, gp_ref))):
        at = slice(part * ROWS, (part + 1) * ROWS)
        grad = own[at, :] + r1[at, :].astype(F32) + r2[at, :].astype(F32) + r3[at, :].astype(F32)
        values = raw[...].astype(F32)
        scale = lax.rsqrt(jnp.sum(values * values, axis=1, keepdims=True) + EPS)
        inner = jnp.sum(values * grad, axis=1, keepdims=True)
        out_ref[...] = scale * grad - values * (inner * scale * scale * scale)


def body(q_embed, p_embed, positives):
    me = lax.axis_index("dev")
    coord = jnp.stack([me // (NZ * NX), (me // NX) % NZ, me % NX]).astype(jnp.int32)
    pos_row = positives.reshape(1, ROWS)
    shape = jax.ShapeDtypeStruct
    packed = shape((SHARD + PAD, WIDTH), BF16)
    stat = shape((16, ROWS), F32)

    own = pl.pallas_call(
        norm_kernel, out_shape=packed, in_specs=[VMEM] * 3, out_specs=VMEM, name="unit_rows"
    )(pos_row, q_embed, p_embed)

    other = shift(own, 0, 1, 0)
    cols0 = [own] + [shift(own, d, 0, 0) for d in range(1, NY)]
    rows = [own] + [shift(own, 0, 0, d) for d in range(1, NX)]
    cols1 = [other] + [shift(other, d, 0, 0) for d in range(1, NY)]

    def forward(first, extra, cols):
        return pl.pallas_call(
            functools.partial(fwd_kernel, first),
            out_shape=[shape((NX * SHARD, NY * SHARD), F32), stat],
            in_specs=[SMEM] + [VMEM] * (len(extra) + NX + NY),
            out_specs=[VMEM, VMEM],
            scratch_shapes=[pltpu.VMEM((NX * SHARD, WIDTH), BF16)],
            compiler_params=params(24),
            cost_estimate=pl.CostEstimate(
                flops=2 * 1024**3, bytes_accessed=8 * 1024**2, transcendentals=1024**2
            ),
            name="scores_first" if first else "scores_second",
        )(coord, *extra, *rows, *cols)

    score0, stat0 = forward(True, [], cols0)
    score1, stat1 = forward(False, [pos_row, stat0], cols1)

    stats = [stat1] + [shift(stat1, 0, 0, d) for d in range(1, NX)]
    joined = pl.pallas_call(
        join_x_kernel,
        out_shape=stat,
        in_specs=[SMEM] + [VMEM] * NX,
        out_specs=VMEM,
        scratch_shapes=[pltpu.VMEM((NX, 8, ROWS), F32), pltpu.VMEM((NX, 8, ROWS), F32)],
        name="join_logs",
    )(coord, *stats)
    pair = jnp.concatenate([joined, shift(joined, 0, 1, 0)], axis=0)
    quads = [pair] + [shift(pair, d, 0, 0) for d in range(1, NY)]
    count = NY * NZ * NX
    lz_rows, lz_cols, ids, loss = pl.pallas_call(
        mid_kernel,
        out_shape=[
            shape((8, ROWS), F32),
            shape((1, NY * NZ * SHARD), F32),
            shape((1, NY * NZ * SHARD), jnp.int32),
            shape((1, ROWS), F32),
        ],
        in_specs=[SMEM] + [VMEM] * NY,
        out_specs=[VMEM] * 4,
        scratch_shapes=[pltpu.VMEM((count + NY * NZ, 8, ROWS), F32)],
        name="log_totals",
    )(coord, *quads)

    def backward(slots, dtype):
        return pl.pallas_call(
            functools.partial(bwd_kernel, slots),
            out_shape=[shape((SHARD, WIDTH), dtype)] * len(slots),
            in_specs=[VMEM] * (5 + NY * NZ),
            out_specs=[VMEM] * len(slots),
            scratch_shapes=[
                pltpu.VMEM((SHARD, NY * NZ * SHARD), BF16),
                pltpu.VMEM((NY * NZ * SHARD, WIDTH), BF16),
            ],
            compiler_params=params(32),
            cost_estimate=pl.CostEstimate(
                flops=len(slots) * 1024**3,
                bytes_accessed=16 * 1024**2,
                transcendentals=len(slots) * 1024**2,
            ),
            name="grads_" + "_".join(str(s) for s in slots),
        )(lz_rows, lz_cols, ids, score0, score1, *cols0, *cols1)

    parts = backward((2, 1, 3), BF16)
    received = [shift(part, 0, 0, -k) for k, part in zip((2, 1, 3), parts)]
    (own_part,) = backward((0,), F32)
    total_rows = ROWS * lax.axis_size("grp") * lax.axis_size("dev")
    mean_loss = lax.psum(loss[0, 0], "grp") / total_rows
    grad_q, grad_p = pl.pallas_call(
        final_kernel,
        out_shape=[shape((ROWS, WIDTH), F32)] * 2,
        in_specs=[VMEM] * 6,
        out_specs=[VMEM] * 2,
        name="pull_back",
    )(own_part, *received, q_embed, p_embed)
    return (mean_loss, grad_q, grad_p)


def solution(mesh):
    return jax.shard_map(
        body,
        mesh=mesh,
        in_specs=(P(("grp", "dev"), None), P(("grp", "dev"), None), P(("grp", "dev"))),
        out_specs=(P(), P(("grp", "dev"), None), P(("grp", "dev"), None)),
        check_vma=False,
    )
```

```python
import functools

import jax
import jax.numpy as jnp
from jax import lax
from jax.experimental import pallas as pl
from jax.experimental.pallas import tpu as pltpu
from jax.sharding import PartitionSpec as P

INV_TEMP = 100.0
EPS = 1e-06
NY, NZ, NX = 4, 2, 4
ROWS = 128
SHARD = 2 * ROWS
PAD = 16
WIDTH = 1024
MASKED = -1e30
F32 = jnp.float32
BF16 = jnp.bfloat16
VMEM = pl.BlockSpec(memory_space=pltpu.VMEM)
SMEM = pl.BlockSpec(memory_space=pltpu.SMEM)
NT = (((1,), (1,)), ((), ()))


def dev_index(core, b, z, a):
    y, x = (a, b) if core else (b, a)
    return (y % NY) * (NZ * NX) + (z % NZ) * NX + x % NX


def shift(value, db, dz, da):
    groups, devs = lax.axis_size("grp"), lax.axis_size("dev")
    pairs = [
        (grp * devs + dev_index(grp % 2, b, z, a), grp * devs + dev_index(grp % 2, b + db, z + dz, a + da))
        for grp in range(groups)
        for b in range(NY)
        for z in range(NZ)
        for a in range(NX)
    ]
    return lax.ppermute(value, ("grp", "dev"), pairs)


def place(core, index):
    high, low = index // (NZ * NX), index % NX
    swap = core == 1
    return jnp.where(swap, low, high), (index // NX) % NZ, jnp.where(swap, high, low)


def slot_of(owner, coord):
    high, low = owner >> 3, owner & 3
    swap = coord[3] == 1
    b, a = jnp.where(swap, low, high), jnp.where(swap, high, low)
    return (coord[0] - b) & 3, ((owner >> 2) & 1) ^ coord[1], (coord[2] - a) & 3


def params(mib):
    return pltpu.CompilerParams(vmem_limit_bytes=mib * 1024 * 1024)


def lse2(left, right):
    top = jnp.maximum(left, right)
    return top + jnp.log(jnp.exp(left - top) + jnp.exp(right - top))


def iota(shape, dim):
    return lax.broadcasted_iota(jnp.int32, shape, dim)


def to_row(column):
    eye = iota((ROWS, ROWS), 0) == iota((ROWS, ROWS), 1)
    return jnp.sum(jnp.where(eye, column, 0.0), axis=0, keepdims=True)


def to_column(row):
    eye = iota((ROWS, ROWS), 0) == iota((ROWS, ROWS), 1)
    return jnp.sum(jnp.where(eye, row, 0.0), axis=1, keepdims=True)


def norm_kernel(pos_ref, q_ref, p_ref, out_ref):
    for part, ref in enumerate((q_ref, p_ref)):
        values = ref[...].astype(F32)
        scale = lax.rsqrt(jnp.sum(values * values, axis=1, keepdims=True) + EPS)
        out_ref[part * ROWS : (part + 1) * ROWS, :] = (values * scale).astype(BF16)
    pos = pos_ref[...]
    high = jnp.broadcast_to((pos >> 6).astype(F32), (PAD, ROWS))
    low = jnp.broadcast_to((pos & 63).astype(F32), (PAD, ROWS))
    out_ref[SHARD:, 0:ROWS] = high.astype(BF16)
    out_ref[SHARD:, ROWS : 2 * ROWS] = low.astype(BF16)
    out_ref[SHARD:, 2 * ROWS :] = jnp.zeros((PAD, WIDTH - 2 * ROWS), BF16)


def fwd_kernel(first, *refs):
    if first:
        coord, *refs = refs
    else:
        coord, pos_ref, before, *refs = refs
    rows, cols = refs[:NX], refs[NX : NX + NY]
    score_ref, stat_ref, col_ref, row_scr = refs[NX + NY :]
    for k in range(NX):
        row_scr[k * SHARD : (k + 1) * SHARD, :] = rows[k][0:SHARD, :]
    for j in range(NY):
        col_ref[j * SHARD : (j + 1) * SHARD, :] = cols[j][0:SHARD, :]
        score_ref[:, j * SHARD : (j + 1) * SHARD] = INV_TEMP * lax.dot_general(
            row_scr[...], cols[j][0:SHARD, :], NT, preferred_element_type=F32
        )

    if first:
        diagonal = iota((SHARD, SHARD), 0) == iota((SHARD, SHARD), 1)
        score_ref[0:SHARD, 0:SHARD] = jnp.where(diagonal, MASKED, score_ref[0:SHARD, 0:SHARD])

    hits = jnp.zeros((ROWS, ROWS), F32)
    for j in range(NY):
        high = cols[j][SHARD : SHARD + PAD, 0:ROWS].astype(F32)[0:1, :]
        low = cols[j][SHARD : SHARD + PAD, ROWS : 2 * ROWS].astype(F32)[0:1, :]
        pos = (high * 64.0 + low).astype(jnp.int32)
        db, dz, da = slot_of(pos >> 7, coord)
        row_id = jnp.where((db == 0) & (dz == 0), da * ROWS + (pos & 127), -1)
        for k in range(NX):
            block = score_ref[
                k * SHARD + ROWS : (k + 1) * SHARD, j * SHARD : j * SHARD + ROWS
            ]
            hit = (iota((ROWS, ROWS), 0) + k * ROWS) == row_id
            hits = hits + jnp.where(hit, block, 0.0)
    hit_row = jnp.sum(hits, axis=0, keepdims=True)

    stat_ref[...] = jnp.zeros_like(stat_ref)

    @pl.loop(0, NX)
    def _(k):
        for part in range(2):
            at = pl.ds(pl.multiple_of(k * SHARD + part * ROWS, ROWS), ROWS)
            block = score_ref[at, :]
            top = jnp.max(block, axis=1, keepdims=True)
            total = jnp.sum(jnp.exp(block - top), axis=1, keepdims=True)
            stat_ref[pl.ds(part * NX + k, 1), :] = to_row(top + jnp.log(total))

    if first:
        stat_ref[8:9, :] = hit_row
    else:
        stat_ref[0:8, :] = lse2(stat_ref[0:8, :], before[0:8, :])
        stat_ref[8:9, :] = hit_row + before[8:9, :]
        stat_ref[9:10, :] = pos_ref[...].astype(F32)


def join_kernel(coord, s0, s1, s2, s3, out_ref, scr, hit_scr):
    a = coord[2]
    stats = (s0, s1, s2, s3)
    for d in range(NX):
        at = (a - d) & 3
        for part in range(2):
            for k in range(NX):
                scr[at, part * NX + k : part * NX + k + 1, :] = stats[d][
                    part * NX + (k - d) % NX : part * NX + (k - d) % NX + 1, :
                ]
        hit_scr[at, 0:1, :] = stats[d][8:9, :]
        out_ref[8 + d : 9 + d, :] = stats[d][9:10, :]
    top = jnp.maximum(jnp.maximum(scr[0], scr[1]), jnp.maximum(scr[2], scr[3]))
    total = jnp.exp(scr[0] - top) + jnp.exp(scr[1] - top)
    total = total + jnp.exp(scr[2] - top) + jnp.exp(scr[3] - top)
    out_ref[0:8, :] = top + jnp.log(total)
    hit = hit_scr[0, 0:1, :] + hit_scr[1, 0:1, :] + hit_scr[2, 0:1, :] + hit_scr[3, 0:1, :]
    out_ref[12:13, :] = hit
    out_ref[13:16, :] = jnp.zeros((3, ROWS), F32)


def mid_kernel(coord, c0, c1, c2, c3, rows_ref, cols_ref, ids_ref, loss_ref, sum_scr):
    parts = (c0, c1, c2, c3)
    count = NY * NZ * NX

    def table(first_row):
        return jnp.concatenate(
            [
                parts[jb][jz * 16 + first_row : jz * 16 + first_row + NX, :]
                for jb in range(NY)
                for jz in range(NZ)
            ],
            axis=0,
        )

    log_b, log_a, pos = table(0), table(4), table(8).astype(jnp.int32)
    lane = pos & 127
    db, dz, da = slot_of(pos >> 7, coord)
    slot = (db * NZ + dz) * NX + da
    log_a_pos = jnp.zeros((count, ROWS), F32)
    for r in range(count):
        picked = jnp.take_along_axis(
            jnp.broadcast_to(log_a[r : r + 1, :], (count, ROWS)), lane, axis=1
        )
        log_a_pos = jnp.where(slot == r, picked, log_a_pos)
    lzq = lse2(log_b, log_a_pos)

    part_high = lzq.astype(BF16).astype(F32)
    part_mid = (lzq - part_high).astype(BF16).astype(F32)
    part_low = lzq - part_high - part_mid
    lane_row = iota((1, ROWS), 1).astype(F32)
    total = jnp.zeros((5 * count, ROWS), F32)
    for group in range(0, count, 2):
        left, right = [], []
        for r in (group, group + 1):
            chosen = iota((count, ROWS), 0) == slot[r : r + 1, :]
            values = (
                part_high[r : r + 1, :],
                part_mid[r : r + 1, :],
                part_low[r : r + 1, :],
                jnp.full((1, ROWS), float(r), F32),
                lane_row,
            )
            left.append(
                jnp.concatenate([jnp.where(chosen, v, 0.0) for v in values], axis=0).astype(BF16)
            )
            right.append((iota((ROWS, ROWS), 0) == lane[r : r + 1, :]).astype(F32).astype(BF16))
        total = total + lax.dot_general(
            jnp.concatenate(left, axis=1),
            jnp.concatenate(right, axis=1),
            NT,
            preferred_element_type=F32,
        )
    lzp = (total[0:count] + total[count : 2 * count]) + total[2 * count : 3 * count]
    from_slot = total[3 * count : 4 * count].astype(jnp.int32)
    from_lane = total[4 * count :].astype(jnp.int32)
    id_q = slot * SHARD + ROWS + lane
    id_p = from_slot * SHARD + from_lane

    rows_ref[0:NX, :] = lzq[0:NX, :]
    rows_ref[NX : 2 * NX, :] = lzp[0:NX, :]
    for jz in range(NZ):
        for jb in range(NY):
            r = (jb * NZ + jz) * NX
            at = (jz * NY + jb) * SHARD
            cols_ref[0:1, at : at + ROWS] = lzq[r : r + 1, :]
            cols_ref[0:1, at + ROWS : at + SHARD] = lzp[r : r + 1, :]
            ids_ref[0:1, at : at + ROWS] = id_q[r : r + 1, :]
            ids_ref[0:1, at + ROWS : at + SHARD] = id_p[r : r + 1, :]

    for jb in range(NY):
        for jz in range(NZ):
            lead = ((coord[0] - jb) & 3) * NZ + (coord[1] ^ jz)
            for ka in range(NX):
                r = (jb * NZ + jz) * NX + ka
                sum_scr[lead * NX + ((coord[2] - ka) & 3), 0:1, :] = lzq[r : r + 1, :]
            sum_scr[count + lead, 0:1, :] = -parts[jb][jz * 16 + 12 : jz * 16 + 13, :]
    row = sum_scr[0, 0:1, :]
    for r in range(1, count + NY * NZ):
        row = row + sum_scr[r, 0:1, :]
    loss_ref[...] = jnp.broadcast_to(jnp.sum(row, axis=1, keepdims=True), (1, ROWS))


def bwd_kernel(k, rows_ref, cols_ref, ids_ref, s0_ref, s1_ref, c0_ref, c1_ref, *refs):
    add_ref, out_ref, g_scr = (refs[-3] if k == 0 else None), refs[-2], refs[-1]
    half_cols = NY * SHARD
    for part in range(2):
        own = to_column(rows_ref[part * NX + k : part * NX + k + 1, :])
        first = k * SHARD + part * ROWS
        for half, score_ref in enumerate((s0_ref, s1_ref)):

            @pl.loop(0, NY * 2)
            def _(j):
                at = pl.ds(pl.multiple_of(j * ROWS, ROWS), ROWS)
                there = pl.ds(pl.multiple_of(half * half_cols + j * ROWS, ROWS), ROWS)
                block = score_ref[first : first + ROWS, at]
                hit = (iota((ROWS, ROWS), 0) + first) == ids_ref[0:1, there]
                grad = jnp.exp(block - own) + jnp.exp(block - cols_ref[0:1, there])
                grad = grad - jnp.where(hit, 1.0, 0.0)
                g_scr[part * ROWS : (part + 1) * ROWS, there] = grad.astype(BF16)

    @pl.loop(0, WIDTH // 256)
    def _(n):
        at = pl.ds(pl.multiple_of(n * 256, 256), 256)
        partial = jnp.dot(g_scr[:, 0:half_cols], c0_ref[:, at], preferred_element_type=F32)
        partial += jnp.dot(g_scr[:, half_cols:], c1_ref[:, at], preferred_element_type=F32)
        partial = partial * INV_TEMP
        if add_ref is not None:
            partial = partial + add_ref[:, at].astype(F32)
        out_ref[:, at] = partial.astype(out_ref.dtype)


def final_kernel(own, r1, r2, q_ref, p_ref, gq_ref, gp_ref):
    for part, (raw, out_ref) in enumerate(((q_ref, gq_ref), (p_ref, gp_ref))):
        at = slice(part * ROWS, (part + 1) * ROWS)
        grad = own[at, :] + r1[at, :].astype(F32) + r2[at, :].astype(F32)
        values = raw[...].astype(F32)
        scale = lax.rsqrt(jnp.sum(values * values, axis=1, keepdims=True) + EPS)
        inner = jnp.sum(values * grad, axis=1, keepdims=True)
        out_ref[...] = scale * grad - values * (inner * scale * scale * scale)


def body(q_embed, p_embed, positives):
    core = lax.axis_index("grp") % 2
    coord = jnp.stack([*place(core, lax.axis_index("dev")), core]).astype(jnp.int32)
    pos_row = positives.reshape(1, ROWS)
    shape = jax.ShapeDtypeStruct
    packed = shape((SHARD + PAD, WIDTH), BF16)
    stat = shape((16, ROWS), F32)

    own = pl.pallas_call(
        norm_kernel, out_shape=packed, in_specs=[VMEM] * 3, out_specs=VMEM,
        compiler_params=params(4), name="unit_rows",
    )(pos_row, q_embed, p_embed)

    other = shift(own, 0, 1, 0)
    b1, b3 = shift(own, 1, 0, 0), shift(own, -1, 0, 0)
    a1, a3 = shift(own, 0, 0, 1), shift(own, 0, 0, -1)
    rows = [own, a1, shift(a1, 0, 0, 1), a3]
    cols0 = [own, b1, shift(b3, -1, 0, 0), b3]
    cols1 = [other, shift(other, 1, 0, 0), shift(other, 2, 0, 0), shift(other, -1, 0, 0)]

    def forward(first, extra, cols):
        return pl.pallas_call(
            functools.partial(fwd_kernel, first),
            out_shape=[
                shape((NX * SHARD, NY * SHARD), F32),
                stat,
                shape((NY * SHARD, WIDTH), BF16),
            ],
            in_specs=[SMEM] + [VMEM] * (len(extra) + NX + NY),
            out_specs=[VMEM] * 3,
            scratch_shapes=[pltpu.VMEM((NX * SHARD, WIDTH), BF16)],
            compiler_params=params(24),
            name="scores_first" if first else "scores_second",
        )(coord, *extra, *rows, *cols)

    score0, stat0, col0 = forward(True, [], cols0)
    score1, stat1, col1 = forward(False, [pos_row, stat0], cols1)

    stats = [stat1] + [shift(stat1, 0, 0, d) for d in range(1, NX)]
    joined = pl.pallas_call(
        join_kernel,
        out_shape=stat,
        in_specs=[SMEM] + [VMEM] * NX,
        out_specs=VMEM,
        scratch_shapes=[pltpu.VMEM((NX, 8, ROWS), F32), pltpu.VMEM((NX, 8, ROWS), F32)],
        compiler_params=params(2),
        name="join_logs",
    )(coord, *stats)
    pair = jnp.concatenate([joined, shift(joined, 0, 1, 0)], axis=0)
    quads = [pair] + [shift(pair, d, 0, 0) for d in range(1, NY)]
    count = NY * NZ * NX
    lz_rows, lz_cols, ids, loss = pl.pallas_call(
        mid_kernel,
        out_shape=[
            shape((8, ROWS), F32),
            shape((1, NY * NZ * SHARD), F32),
            shape((1, NY * NZ * SHARD), jnp.int32),
            shape((1, ROWS), F32),
        ],
        in_specs=[SMEM] + [VMEM] * NY,
        out_specs=[VMEM] * 4,
        scratch_shapes=[pltpu.VMEM((count + NY * NZ, 8, ROWS), F32)],
        compiler_params=params(4),
        name="log_totals",
    )(coord, *quads)

    def backward(k, dtype, *extra):
        return pl.pallas_call(
            functools.partial(bwd_kernel, k),
            out_shape=shape((SHARD, WIDTH), dtype),
            in_specs=[VMEM] * (7 + len(extra)),
            out_specs=VMEM,
            scratch_shapes=[pltpu.VMEM((SHARD, NY * NZ * SHARD), BF16)],
            compiler_params=params(20),
            name="grads_" + str(k),
        )(lz_rows, lz_cols, ids, score0, score1, col0, col1, *extra)

    groups = lax.axis_size("grp")

    def add_over(value, step):
        return value + lax.ppermute(value, "grp", [(g, g ^ step) for g in range(groups)])

    part2 = shift(backward(2, BF16), 0, 0, -2)
    part1 = shift(backward(1, BF16), 0, 0, -1)
    loss = add_over(loss, 1)
    part3 = shift(backward(3, BF16, loss), 0, 0, -3)
    loss = add_over(loss, 2)
    own_part = backward(0, F32, loss, part2)
    loss = add_over(loss, 4)
    mean_loss = loss[0, 0] / (ROWS * groups * lax.axis_size("dev"))
    grad_q, grad_p = pl.pallas_call(
        final_kernel,
        out_shape=[shape((ROWS, WIDTH), F32)] * 2,
        in_specs=[VMEM] * 5,
        out_specs=[VMEM] * 2,
        compiler_params=params(16),
        name="pull_back",
    )(own_part, part1, part3, q_embed, p_embed)
    return (mean_loss, grad_q, grad_p)


def solution(mesh):
    return jax.shard_map(
        body,
        mesh=mesh,
        in_specs=(P(("grp", "dev"), None), P(("grp", "dev"), None), P(("grp", "dev"))),
        out_specs=(P(), P(("grp", "dev"), None), P(("grp", "dev"), None)),
        check_vma=False,
    )
```

```python
import functools

import jax
import jax.numpy as jnp
from jax import lax
from jax.experimental import pallas as pl
from jax.experimental.pallas import tpu as pltpu
from jax.sharding import PartitionSpec as P

INV_TEMP = 100.0
EPS = 1e-06
NY, NZ, NX = 4, 2, 4
ROWS = 128
SHARD = 2 * ROWS
PAD = 16
WIDTH = 1024
STRIP = 32
MASKED = -1e30
F32 = jnp.float32
BF16 = jnp.bfloat16
VMEM = pl.BlockSpec(memory_space=pltpu.VMEM)
ANY = pl.BlockSpec(memory_space=pl.ANY)
HBM = pl.BlockSpec(memory_space=pltpu.HBM)
SMEM = pl.BlockSpec(memory_space=pltpu.SMEM)
NT = (((1,), (1,)), ((), ()))


def dev_index(core, b, z, a):
    y, x = (a, b) if core else (b, a)
    return (y % NY) * (NZ * NX) + (z % NZ) * NX + x % NX


def shift(value, db, dz, da):
    groups, devs = lax.axis_size("grp"), lax.axis_size("dev")
    pairs = [
        (grp * devs + dev_index(grp % 2, b, z, a), grp * devs + dev_index(grp % 2, b + db, z + dz, a + da))
        for grp in range(groups)
        for b in range(NY)
        for z in range(NZ)
        for a in range(NX)
    ]
    return lax.ppermute(value, ("grp", "dev"), pairs)


def place(core, index):
    high, low = index // (NZ * NX), index % NX
    swap = core == 1
    return jnp.where(swap, low, high), (index // NX) % NZ, jnp.where(swap, high, low)


def slot_of(owner, coord):
    high, low = owner >> 3, owner & 3
    swap = coord[3] == 1
    b, a = jnp.where(swap, low, high), jnp.where(swap, high, low)
    return (coord[0] - b) & 3, ((owner >> 2) & 1) ^ coord[1], (coord[2] - a) & 3


def params(mib):
    return pltpu.CompilerParams(vmem_limit_bytes=mib * 1024 * 1024)


def lse2(left, right):
    top = jnp.maximum(left, right)
    return top + jnp.log(jnp.exp(left - top) + jnp.exp(right - top))


def iota(shape, dim):
    return lax.broadcasted_iota(jnp.int32, shape, dim)


def to_row(column):
    eye = iota((ROWS, ROWS), 0) == iota((ROWS, ROWS), 1)
    return jnp.sum(jnp.where(eye, column, 0.0), axis=0, keepdims=True)


def to_column(row):
    eye = iota((ROWS, ROWS), 0) == iota((ROWS, ROWS), 1)
    return jnp.sum(jnp.where(eye, row, 0.0), axis=1, keepdims=True)


def norm_kernel(pos_hbm, q_hbm, p_hbm, out_ref, plain_ref, pos_ref, raw_ref, sems):
    copies = [
        pltpu.make_async_copy(q_hbm, raw_ref.at[0], sems.at[0]),
        pltpu.make_async_copy(p_hbm, raw_ref.at[1], sems.at[1]),
        pltpu.make_async_copy(pos_hbm, pos_ref, sems.at[2]),
    ]
    for copy in copies:
        copy.start()
    for part in range(2):
        copies[part].wait()
        values = raw_ref[part].astype(F32)
        scale = lax.rsqrt(jnp.sum(values * values, axis=1, keepdims=True) + EPS)
        unit = (values * scale).astype(BF16)
        out_ref[part * ROWS : (part + 1) * ROWS, :] = unit
        plain_ref[part * ROWS : (part + 1) * ROWS, :] = unit
    copies[2].wait()
    pos = pos_ref[...]
    high = jnp.broadcast_to((pos >> 6).astype(F32), (PAD, ROWS))
    low = jnp.broadcast_to((pos & 63).astype(F32), (PAD, ROWS))
    out_ref[SHARD:, 0:ROWS] = high.astype(BF16)
    out_ref[SHARD:, ROWS : 2 * ROWS] = low.astype(BF16)
    out_ref[SHARD:, 2 * ROWS :] = jnp.zeros((PAD, WIDTH - 2 * ROWS), BF16)


def gate_kernel(*refs):
    del refs


def fwd_kernel(stage, col_counts, *refs):
    if stage < 2:
        coord, *refs = refs
    else:
        coord, before, between, pos_ref, *refs = refs
    parts = len(col_counts)
    rows, cols = refs[:NX], refs[NX : NX + parts]
    score_ref, stat_ref, col_ref, row_scr = refs[NX + parts :]
    for k in range(NX):
        row_scr[k * SHARD : (k + 1) * SHARD, :] = rows[k][0:SHARD, :]
    at = 0
    for ref, count in zip(cols, col_counts):
        col_ref[at : at + count, :] = ref[...]
        at += count
    for at in range(0, sum(col_counts), 256):
        score_ref[:, at : at + 256] = INV_TEMP * lax.dot_general(
            row_scr[...], col_ref[at : at + 256, :], NT, preferred_element_type=F32
        )

    stat_ref[...] = jnp.zeros_like(stat_ref)
    if stage == 0:
        diagonal = iota((SHARD, SHARD), 0) == iota((SHARD, SHARD), 1)
        score_ref[0:SHARD, 0:SHARD] = jnp.where(diagonal, MASKED, score_ref[0:SHARD, 0:SHARD])

    lead_slot = 2 if stage == 2 else 0
    hits = jnp.zeros((ROWS, ROWS), F32)
    for k in range(NX):
        high = rows[k][SHARD : SHARD + PAD, 0:ROWS].astype(F32)[0:1, :]
        low = rows[k][SHARD : SHARD + PAD, ROWS : 2 * ROWS].astype(F32)[0:1, :]
        pos = (high * 64.0 + low).astype(jnp.int32)
        db, dz, da = slot_of(pos >> 7, coord)
        here = (dz == (1 if stage else 0)) & (da == 0)
        place_row = jnp.where(here, db * ROWS + (pos & 127), -1)
        col_id = to_column(place_row.astype(F32)).astype(jnp.int32)
        for j in range(parts):
            lead = j * SHARD + ROWS
            block = score_ref[k * SHARD : k * SHARD + ROWS, lead : lead + ROWS]
            hit = (iota((ROWS, ROWS), 1) + (lead_slot + j) * ROWS) == col_id
            hits = hits + jnp.where(hit, block, 0.0)
    stat_ref[8:9, :] = jnp.sum(hits, axis=0, keepdims=True)

    @pl.loop(0, NX)
    def _(k):
        for part in range(2):
            at = pl.ds(pl.multiple_of(k * SHARD + part * ROWS, ROWS), ROWS)
            block = score_ref[at, :]
            top = jnp.max(block, axis=1, keepdims=True)
            total = jnp.sum(jnp.exp(block - top), axis=1, keepdims=True)
            stat_ref[pl.ds(part * NX + k, 1), :] = to_row(top + jnp.log(total))

    if stage == 2:
        stat_ref[0:8, :] = lse2(lse2(stat_ref[0:8, :], between[0:8, :]), before[0:8, :])
        stat_ref[8:9, :] = stat_ref[8:9, :] + (between[8:9, :] + before[8:9, :])
        stat_ref[9:10, :] = pos_ref[...].astype(F32)


def join_kernel(coord, s0, s1, s2, s3, out_ref, scr, hit_scr):
    a = coord[2]
    stats = (s0, s1, s2, s3)
    for d in range(NX):
        at = (a - d) & 3
        for part in range(2):
            for k in range(NX):
                scr[at, part * NX + k : part * NX + k + 1, :] = stats[d][
                    part * NX + (k - d) % NX : part * NX + (k - d) % NX + 1, :
                ]
        hit_scr[at, 0:1, :] = stats[d][8:9, :]
        out_ref[8 + d : 9 + d, :] = stats[d][9:10, :]
    top = jnp.maximum(jnp.maximum(scr[0], scr[1]), jnp.maximum(scr[2], scr[3]))
    total = jnp.exp(scr[0] - top) + jnp.exp(scr[1] - top)
    total = total + jnp.exp(scr[2] - top) + jnp.exp(scr[3] - top)
    out_ref[0:8, :] = top + jnp.log(total)
    hit = hit_scr[0, 0:1, :] + hit_scr[1, 0:1, :] + hit_scr[2, 0:1, :] + hit_scr[3, 0:1, :]
    out_ref[12:13, :] = hit
    out_ref[13:16, :] = jnp.zeros((3, ROWS), F32)


def mid_kernel(coord, c0, c1, c2, c3, rows_ref, cols_ref, ids_ref, loss_ref, sum_scr):
    parts = (c0, c1, c2, c3)
    count = NY * NZ * NX

    def table(first_row):
        return jnp.concatenate(
            [
                parts[jb][jz * 16 + first_row : jz * 16 + first_row + NX, :]
                for jb in range(NY)
                for jz in range(NZ)
            ],
            axis=0,
        )

    log_b, log_a, pos = table(0), table(4), table(8).astype(jnp.int32)
    lane = pos & 127
    db, dz, da = slot_of(pos >> 7, coord)
    slot = (db * NZ + dz) * NX + da
    log_a_pos = jnp.zeros((count, ROWS), F32)
    for r in range(count):
        picked = jnp.take_along_axis(
            jnp.broadcast_to(log_a[r : r + 1, :], (count, ROWS)), lane, axis=1
        )
        log_a_pos = jnp.where(slot == r, picked, log_a_pos)
    lzq = lse2(log_b, log_a_pos)

    part_high = lzq.astype(BF16).astype(F32)
    part_mid = (lzq - part_high).astype(BF16).astype(F32)
    part_low = lzq - part_high - part_mid
    lane_row = iota((1, ROWS), 1).astype(F32)
    total = jnp.zeros((5 * count, ROWS), F32)
    for group in range(0, count, 2):
        left, right = [], []
        for r in (group, group + 1):
            chosen = iota((count, ROWS), 0) == slot[r : r + 1, :]
            values = (
                part_high[r : r + 1, :],
                part_mid[r : r + 1, :],
                part_low[r : r + 1, :],
                jnp.full((1, ROWS), float(r), F32),
                lane_row,
            )
            left.append(
                jnp.concatenate([jnp.where(chosen, v, 0.0) for v in values], axis=0).astype(BF16)
            )
            right.append((iota((ROWS, ROWS), 0) == lane[r : r + 1, :]).astype(F32).astype(BF16))
        total = total + lax.dot_general(
            jnp.concatenate(left, axis=1),
            jnp.concatenate(right, axis=1),
            NT,
            preferred_element_type=F32,
        )
    lzp = (total[0:count] + total[count : 2 * count]) + total[2 * count : 3 * count]
    from_slot = total[3 * count : 4 * count].astype(jnp.int32)
    from_lane = total[4 * count :].astype(jnp.int32)
    id_q = slot * SHARD + ROWS + lane
    id_p = from_slot * SHARD + from_lane

    rows_ref[0:NX, :] = lzq[0:NX, :]
    rows_ref[NX : 2 * NX, :] = lzp[0:NX, :]
    for jb in range(NY):
        for jz in range(NZ):
            r = (jb * NZ + jz) * NX
            at = (jz * NY + jb) * SHARD
            for part, (lz, ids) in enumerate(((lzq, id_q), (lzp, id_p))):
                here = slice(at + part * ROWS, at + (part + 1) * ROWS)
                cols_ref[0:1, here] = lz[r : r + 1, :]
                ids_ref[0:1, here] = ids[r : r + 1, :]

    for jb in range(NY):
        for jz in range(NZ):
            lead = ((coord[0] - jb) & 3) * NZ + (coord[1] ^ jz)
            for ka in range(NX):
                r = (jb * NZ + jz) * NX + ka
                sum_scr[lead * NX + ((coord[2] - ka) & 3), 0:1, :] = lzq[r : r + 1, :]
            sum_scr[count + lead, 0:1, :] = -parts[jb][jz * 16 + 12 : jz * 16 + 13, :]
    row = sum_scr[0, 0:1, :]
    for r in range(1, count + NY * NZ):
        row = row + sum_scr[r, 0:1, :]
    loss_ref[...] = jnp.broadcast_to(jnp.sum(row, axis=1, keepdims=True), (1, ROWS))


def bwd_kernel(k, rows_ref, cols_ref, ids_ref, *refs):
    scores, cols = refs[0:3], refs[3:6]
    add_ref, out_ref, g_scr, own_scr = (refs[-4] if k == 0 else None), *refs[-3:]
    for part in range(2):
        own = to_column(rows_ref[part * NX + k : part * NX + k + 1, :])
        own_scr[part * ROWS : (part + 1) * ROWS, :] = jnp.broadcast_to(own, (ROWS, ROWS))

    @pl.loop(0, SHARD // STRIP)
    def _(r):
        at = pl.ds(pl.multiple_of(r * STRIP, STRIP), STRIP)
        there = pl.ds(pl.multiple_of(k * SHARD + r * STRIP, STRIP), STRIP)
        own = own_scr[at, :]
        row_id = iota((STRIP, ROWS), 0) + (k * SHARD + r * STRIP)
        start = 0
        for score_ref in scores:
            for c in range(0, score_ref.shape[1], ROWS):
                lanes = slice(start + c, start + c + ROWS)
                block = score_ref[there, c : c + ROWS]
                grad = jnp.exp(block - own) + jnp.exp(block - cols_ref[0:1, lanes])
                grad = grad - jnp.where(row_id == ids_ref[0:1, lanes], 1.0, 0.0)
                g_scr[at, lanes] = grad.astype(BF16)
            start += score_ref.shape[1]

    for n in range(0, WIDTH, 256):
        at = slice(n, n + 256)
        partial, start = 0.0, 0
        for ref in cols:
            part = g_scr[:, start : start + ref.shape[0]]
            partial += jnp.dot(part, ref[:, at], preferred_element_type=F32)
            start += ref.shape[0]
        partial = partial * INV_TEMP
        if add_ref is not None:
            partial = partial + add_ref[:, at].astype(F32)
        out_ref[:, at] = partial.astype(out_ref.dtype)


def final_kernel(own, r1, r2, q_ref, p_ref, gq_ref, gp_ref):
    for part, (raw, out_ref) in enumerate(((q_ref, gq_ref), (p_ref, gp_ref))):
        at = slice(part * ROWS, (part + 1) * ROWS)
        grad = own[at, :] + r1[at, :].astype(F32) + r2[at, :].astype(F32)
        values = raw[...].astype(F32)
        scale = lax.rsqrt(jnp.sum(values * values, axis=1, keepdims=True) + EPS)
        inner = jnp.sum(values * grad, axis=1, keepdims=True)
        out_ref[...] = scale * grad - values * (inner * scale * scale * scale)


def body(q_embed, p_embed, positives):
    core = lax.axis_index("grp") % 2
    coord = jnp.stack([*place(core, lax.axis_index("dev")), core]).astype(jnp.int32)
    pos_row = positives.reshape(1, ROWS)
    shape = jax.ShapeDtypeStruct
    packed = shape((SHARD + PAD, WIDTH), BF16)
    stat = shape((16, ROWS), F32)

    own, plain = pl.pallas_call(
        norm_kernel,
        out_shape=[packed, shape((SHARD, WIDTH), BF16)],
        in_specs=[HBM] * 3,
        out_specs=[VMEM] * 2,
        scratch_shapes=[
            pltpu.VMEM((1, ROWS), jnp.int32),
            pltpu.VMEM((2, ROWS, WIDTH), BF16),
            pltpu.SemaphoreType.DMA((3,)),
        ],
        compiler_params=params(60),
        name="unit_rows",
    )(pos_row, q_embed, p_embed)

    def gate(value, *others):
        return pl.pallas_call(
            gate_kernel,
            out_shape=shape(value.shape, value.dtype),
            in_specs=[ANY] * (1 + len(others)),
            out_specs=ANY,
            input_output_aliases={0: 0},
            compiler_params=params(1),
            name="gate",
        )(value, *others)

    far = shift(own, 0, 1, 0)[:SHARD]
    b1, b3 = shift(plain, 1, 0, 0), shift(plain, -1, 0, 0)
    a1, a3 = shift(own, 0, 0, 1), shift(own, 0, 0, -1)
    rows = [own, a1, shift(a1, 0, 0, 1), a3]
    cols = [plain, b1, shift(b3, -1, 0, 0), b3]
    far = gate(far, rows[2], cols[2])
    far_cols = [far] + [shift(far, d, 0, 0) for d in (1, 2, -1)]

    def forward(stage, extra, cols):
        counts = tuple(c.shape[0] for c in cols)
        return pl.pallas_call(
            functools.partial(fwd_kernel, stage, counts),
            out_shape=[
                shape((NX * SHARD, sum(counts)), F32),
                stat,
                shape((sum(counts), WIDTH), BF16),
            ],
            in_specs=[SMEM] + [VMEM] * (len(extra) + NX + len(cols)),
            out_specs=[VMEM] * 3,
            scratch_shapes=[pltpu.VMEM((NX * SHARD, WIDTH), BF16)],
            compiler_params=params(20),
            name="scores_" + str(stage),
        )(coord, *extra, *rows, *cols)

    score0, stat0, col0 = forward(0, [], cols)
    score1, stat1, col1 = forward(1, [], far_cols[:2])
    score2, stat1, col2 = forward(2, [stat0, stat1, pos_row], far_cols[2:])

    stats = [stat1] + [shift(stat1, 0, 0, d) for d in range(1, NX)]
    joined = pl.pallas_call(
        join_kernel,
        out_shape=stat,
        in_specs=[SMEM] + [VMEM] * NX,
        out_specs=VMEM,
        scratch_shapes=[pltpu.VMEM((NX, 8, ROWS), F32), pltpu.VMEM((NX, 8, ROWS), F32)],
        compiler_params=params(2),
        name="join_logs",
    )(coord, *stats)
    pair = jnp.concatenate([joined, shift(joined, 0, 1, 0)], axis=0)
    quads = [pair] + [shift(pair, d, 0, 0) for d in range(1, NY)]
    count = NY * NZ * NX
    lz_rows, lz_cols, ids, loss = pl.pallas_call(
        mid_kernel,
        out_shape=[
            shape((2 * NX, ROWS), F32),
            shape((1, NY * NZ * SHARD), F32),
            shape((1, NY * NZ * SHARD), jnp.int32),
            shape((1, ROWS), F32),
        ],
        in_specs=[SMEM] + [VMEM] * NY,
        out_specs=[VMEM] * 4,
        scratch_shapes=[pltpu.VMEM((count + NY * NZ, 8, ROWS), F32)],
        compiler_params=params(4),
        name="log_totals",
    )(coord, *quads)

    def backward(k, dtype, *extra):
        return pl.pallas_call(
            functools.partial(bwd_kernel, k),
            out_shape=shape((SHARD, WIDTH), dtype),
            in_specs=[VMEM] * (9 + len(extra)),
            out_specs=VMEM,
            scratch_shapes=[
                pltpu.VMEM((SHARD, NY * NZ * SHARD), BF16),
                pltpu.VMEM((SHARD, ROWS), F32),
            ],
            compiler_params=params(20),
            cost_estimate=pl.CostEstimate(
                flops=2 * 1024**3, bytes_accessed=6 * 1024**2, transcendentals=1024**2
            ),
            name="grads_" + str(k),
        )(lz_rows, lz_cols, ids, score0, score1, score2, col0, col1, col2, *extra)

    groups = lax.axis_size("grp")

    def add_over(value, step):
        return value + lax.ppermute(value, "grp", [(g, g ^ step) for g in range(groups)])

    part2 = shift(backward(2, BF16), 0, 0, -2)
    loss = add_over(loss, 1)
    part1 = shift(backward(1, BF16, loss), 0, 0, -1)
    loss = add_over(loss, 2)
    part3 = shift(backward(3, BF16, loss), 0, 0, -3)
    loss = add_over(loss, 4)
    own_part = backward(0, F32, loss, part2)
    mean_loss = loss[0, 0] / (ROWS * groups * lax.axis_size("dev"))
    grad_q, grad_p = pl.pallas_call(
        final_kernel,
        out_shape=[shape((ROWS, WIDTH), F32)] * 2,
        in_specs=[VMEM] * 5,
        out_specs=[VMEM] * 2,
        compiler_params=params(16),
        name="pull_back",
    )(own_part, part1, part3, q_embed, p_embed)
    return (mean_loss, grad_q, grad_p)


def solution(mesh):
    return jax.shard_map(
        body,
        mesh=mesh,
        in_specs=(P(("grp", "dev"), None), P(("grp", "dev"), None), P(("grp", "dev"))),
        out_specs=(P(), P(("grp", "dev"), None), P(("grp", "dev"), None)),
        check_vma=False,
    )
```

```python
import functools

import jax
import jax.numpy as jnp
from jax import lax
from jax.experimental import pallas as pl
from jax.experimental.pallas import tpu as pltpu
from jax.sharding import PartitionSpec as P

INV_TEMP = 100.0
EPS = 1e-06
NY, NZ, NX = 4, 2, 4
ROWS = 128
SHARD = 2 * ROWS
PAD = 16
WIDTH = 1024
STRIP = 32
MASKED = -1e30
F32 = jnp.float32
BF16 = jnp.bfloat16
VMEM = pl.BlockSpec(memory_space=pltpu.VMEM)
ANY = pl.BlockSpec(memory_space=pl.ANY)
HBM = pl.BlockSpec(memory_space=pltpu.HBM)
SMEM = pl.BlockSpec(memory_space=pltpu.SMEM)
NT = (((1,), (1,)), ((), ()))


def dev_index(core, b, z, a):
    y, x = (a, b) if core else (b, a)
    return (y % NY) * (NZ * NX) + (z % NZ) * NX + x % NX


def shift(value, db, dz, da):
    groups, devs = lax.axis_size("grp"), lax.axis_size("dev")
    pairs = [
        (grp * devs + dev_index(grp % 2, b, z, a), grp * devs + dev_index(grp % 2, b + db, z + dz, a + da))
        for grp in range(groups)
        for b in range(NY)
        for z in range(NZ)
        for a in range(NX)
    ]
    return lax.ppermute(value, ("grp", "dev"), pairs)


def place(core, index):
    high, low = index // (NZ * NX), index % NX
    swap = core == 1
    return jnp.where(swap, low, high), (index // NX) % NZ, jnp.where(swap, high, low)


def slot_of(owner, coord):
    high, low = owner >> 3, owner & 3
    swap = coord[3] == 1
    b, a = jnp.where(swap, low, high), jnp.where(swap, high, low)
    return (coord[0] - b) & 3, ((owner >> 2) & 1) ^ coord[1], (coord[2] - a) & 3


def params(mib):
    return pltpu.CompilerParams(vmem_limit_bytes=mib * 1024 * 1024)


def lse2(left, right):
    top = jnp.maximum(left, right)
    return top + jnp.log(jnp.exp(left - top) + jnp.exp(right - top))


def iota(shape, dim):
    return lax.broadcasted_iota(jnp.int32, shape, dim)


def to_row(column):
    eye = iota((ROWS, ROWS), 0) == iota((ROWS, ROWS), 1)
    return jnp.sum(jnp.where(eye, column, 0.0), axis=0, keepdims=True)


def to_column(row):
    eye = iota((ROWS, ROWS), 0) == iota((ROWS, ROWS), 1)
    return jnp.sum(jnp.where(eye, row, 0.0), axis=1, keepdims=True)


def norm_kernel(pos_hbm, q_hbm, p_hbm, out_ref, plain_ref, pos_ref, raw_ref, sems):
    copies = [
        pltpu.make_async_copy(q_hbm, raw_ref.at[0], sems.at[0]),
        pltpu.make_async_copy(p_hbm, raw_ref.at[1], sems.at[1]),
        pltpu.make_async_copy(pos_hbm, pos_ref, sems.at[2]),
    ]
    for copy in copies:
        copy.start()
    for part in range(2):
        copies[part].wait()
        values = raw_ref[part].astype(F32)
        scale = lax.rsqrt(jnp.sum(values * values, axis=1, keepdims=True) + EPS)
        unit = (values * scale).astype(BF16)
        out_ref[part * ROWS : (part + 1) * ROWS, :] = unit
        plain_ref[part * ROWS : (part + 1) * ROWS, :] = unit
    copies[2].wait()
    pos = pos_ref[...]
    high = jnp.broadcast_to((pos >> 6).astype(F32), (PAD, ROWS))
    low = jnp.broadcast_to((pos & 63).astype(F32), (PAD, ROWS))
    out_ref[SHARD:, 0:ROWS] = high.astype(BF16)
    out_ref[SHARD:, ROWS : 2 * ROWS] = low.astype(BF16)
    out_ref[SHARD:, 2 * ROWS :] = jnp.zeros((PAD, WIDTH - 2 * ROWS), BF16)


def gate_kernel(*refs):
    del refs


def fwd_kernel(stage, col_counts, *refs):
    if stage < 2:
        coord, *refs = refs
    else:
        coord, before, between, pos_ref, *refs = refs
    parts = len(col_counts)
    if stage == 0:
        rows, cols = refs[:NX], refs[NX : NX + parts]
        score_ref, stat_ref, col_ref, row_ref, place_ref = refs[NX + parts :]
        for k in range(NX):
            row_ref[k * SHARD : (k + 1) * SHARD, :] = rows[k][0:SHARD, :]
            digits = rows[k][SHARD : SHARD + PAD, 0 : 2 * ROWS].astype(F32)
            place_ref[k : k + 1, :] = (digits[0:1, 0:ROWS] * 64.0 + digits[0:1, ROWS:]).astype(
                jnp.int32
            )
        place_ref[NX:, :] = jnp.zeros((8 - NX, ROWS), jnp.int32)
    else:
        row_ref, place_ref, *cols = refs[: 2 + parts]
        score_ref, stat_ref, col_ref = refs[2 + parts :]
    at = 0
    for ref, count in zip(cols, col_counts):
        col_ref[at : at + count, :] = ref[...]
        at += count
    stat_ref[...] = jnp.zeros_like(stat_ref)
    for k in range(NX):
        chunk = slice(k * SHARD, (k + 1) * SHARD)
        block = INV_TEMP * lax.dot_general(
            row_ref[chunk, :], col_ref[...], NT, preferred_element_type=F32
        )
        score_ref[chunk, :] = block
        if stage == 0 and k == 0:
            diagonal = iota((SHARD, SHARD), 0) == iota((SHARD, SHARD), 1)
            score_ref[chunk, 0:SHARD] = jnp.where(diagonal, MASKED, score_ref[chunk, 0:SHARD])
        for part in range(2):
            first = k * SHARD + part * ROWS
            block = score_ref[first : first + ROWS, :]
            top = jnp.max(block, axis=1, keepdims=True)
            total = jnp.sum(jnp.exp(block - top), axis=1, keepdims=True)
            lead = part * NX + k
            stat_ref[lead : lead + 1, :] = to_row(top + jnp.log(total))

    lead_slot = 2 if stage == 2 else 0
    hits = jnp.zeros((ROWS, ROWS), F32)
    for k in range(NX):
        pos = place_ref[k : k + 1, :]
        db, dz, da = slot_of(pos >> 7, coord)
        here = (dz == (1 if stage else 0)) & (da == 0)
        place_row = jnp.where(here, db * ROWS + (pos & 127), -1)
        col_id = to_column(place_row.astype(F32)).astype(jnp.int32)
        for j in range(parts):
            lead = j * SHARD + ROWS
            block = score_ref[k * SHARD : k * SHARD + ROWS, lead : lead + ROWS]
            hit = (iota((ROWS, ROWS), 1) + (lead_slot + j) * ROWS) == col_id
            hits = hits + jnp.where(hit, block, 0.0)
    stat_ref[8:9, :] = jnp.sum(hits, axis=0, keepdims=True)

    if stage == 2:
        stat_ref[0:8, :] = lse2(lse2(stat_ref[0:8, :], between[0:8, :]), before[0:8, :])
        stat_ref[8:9, :] = stat_ref[8:9, :] + (between[8:9, :] + before[8:9, :])
        stat_ref[9:10, :] = pos_ref[...].astype(F32)


def join_kernel(coord, s0, s1, s2, s3, out_ref, scr, hit_scr):
    a = coord[2]
    stats = (s0, s1, s2, s3)
    for d in range(NX):
        at = (a - d) & 3
        for part in range(2):
            for k in range(NX):
                scr[at, part * NX + k : part * NX + k + 1, :] = stats[d][
                    part * NX + (k - d) % NX : part * NX + (k - d) % NX + 1, :
                ]
        hit_scr[at, 0:1, :] = stats[d][8:9, :]
        out_ref[8 + d : 9 + d, :] = stats[d][9:10, :]
    top = jnp.maximum(jnp.maximum(scr[0], scr[1]), jnp.maximum(scr[2], scr[3]))
    total = jnp.exp(scr[0] - top) + jnp.exp(scr[1] - top)
    total = total + jnp.exp(scr[2] - top) + jnp.exp(scr[3] - top)
    out_ref[0:8, :] = top + jnp.log(total)
    hit = hit_scr[0, 0:1, :] + hit_scr[1, 0:1, :] + hit_scr[2, 0:1, :] + hit_scr[3, 0:1, :]
    out_ref[12:13, :] = hit
    out_ref[13:16, :] = jnp.zeros((3, ROWS), F32)


def mid_kernel(coord, c0, c1, c2, c3, rows_ref, cols_ref, ids_ref, loss_ref, sum_scr):
    parts = (c0, c1, c2, c3)
    count = NY * NZ * NX

    def table(first_row):
        return jnp.concatenate(
            [
                parts[jb][jz * 16 + first_row : jz * 16 + first_row + NX, :]
                for jb in range(NY)
                for jz in range(NZ)
            ],
            axis=0,
        )

    log_b, log_a, pos = table(0), table(4), table(8).astype(jnp.int32)
    lane = pos & 127
    db, dz, da = slot_of(pos >> 7, coord)
    slot = (db * NZ + dz) * NX + da
    log_a_pos = jnp.zeros((count, ROWS), F32)
    for r in range(count):
        picked = jnp.take_along_axis(
            jnp.broadcast_to(log_a[r : r + 1, :], (count, ROWS)), lane, axis=1
        )
        log_a_pos = jnp.where(slot == r, picked, log_a_pos)
    lzq = lse2(log_b, log_a_pos)

    part_high = lzq.astype(BF16).astype(F32)
    part_mid = (lzq - part_high).astype(BF16).astype(F32)
    part_low = lzq - part_high - part_mid
    lane_row = iota((1, ROWS), 1).astype(F32)
    total = jnp.zeros((5 * count, ROWS), F32)
    for group in range(0, count, 2):
        left, right = [], []
        for r in (group, group + 1):
            chosen = iota((count, ROWS), 0) == slot[r : r + 1, :]
            values = (
                part_high[r : r + 1, :],
                part_mid[r : r + 1, :],
                part_low[r : r + 1, :],
                jnp.full((1, ROWS), float(r), F32),
                lane_row,
            )
            left.append(
                jnp.concatenate([jnp.where(chosen, v, 0.0) for v in values], axis=0).astype(BF16)
            )
            right.append((iota((ROWS, ROWS), 0) == lane[r : r + 1, :]).astype(F32).astype(BF16))
        total = total + lax.dot_general(
            jnp.concatenate(left, axis=1),
            jnp.concatenate(right, axis=1),
            NT,
            preferred_element_type=F32,
        )
    lzp = (total[0:count] + total[count : 2 * count]) + total[2 * count : 3 * count]
    from_slot = total[3 * count : 4 * count].astype(jnp.int32)
    from_lane = total[4 * count :].astype(jnp.int32)
    id_q = slot * SHARD + ROWS + lane
    id_p = from_slot * SHARD + from_lane

    rows_ref[0:NX, :] = lzq[0:NX, :]
    rows_ref[NX : 2 * NX, :] = lzp[0:NX, :]
    for jb in range(NY):
        for jz in range(NZ):
            r = (jb * NZ + jz) * NX
            at = (jz * NY + jb) * SHARD
            for part, (lz, ids) in enumerate(((lzq, id_q), (lzp, id_p))):
                here = slice(at + part * ROWS, at + (part + 1) * ROWS)
                cols_ref[0:1, here] = lz[r : r + 1, :]
                ids_ref[0:1, here] = ids[r : r + 1, :]

    for jb in range(NY):
        for jz in range(NZ):
            lead = ((coord[0] - jb) & 3) * NZ + (coord[1] ^ jz)
            for ka in range(NX):
                r = (jb * NZ + jz) * NX + ka
                sum_scr[lead * NX + ((coord[2] - ka) & 3), 0:1, :] = lzq[r : r + 1, :]
            sum_scr[count + lead, 0:1, :] = -parts[jb][jz * 16 + 12 : jz * 16 + 13, :]
    row = sum_scr[0, 0:1, :]
    for r in range(1, count + NY * NZ):
        row = row + sum_scr[r, 0:1, :]
    loss_ref[...] = jnp.broadcast_to(jnp.sum(row, axis=1, keepdims=True), (1, ROWS))


def bwd_kernel(k, rows_ref, cols_ref, ids_ref, *refs):
    scores, cols = refs[0:3], refs[3:6]
    add_ref, out_ref, g_scr, own_scr = (refs[-4] if k == 0 else None), *refs[-3:]
    for part in range(2):
        own = to_column(rows_ref[part * NX + k : part * NX + k + 1, :])
        own_scr[part * ROWS : (part + 1) * ROWS, :] = jnp.broadcast_to(own, (ROWS, ROWS))

    @pl.loop(0, SHARD // STRIP)
    def _(r):
        at = pl.ds(pl.multiple_of(r * STRIP, STRIP), STRIP)
        there = pl.ds(pl.multiple_of(k * SHARD + r * STRIP, STRIP), STRIP)
        own = own_scr[at, :]
        row_id = iota((STRIP, ROWS), 0) + (k * SHARD + r * STRIP)
        start = 0
        for score_ref in scores:
            for c in range(0, score_ref.shape[1], ROWS):
                lanes = slice(start + c, start + c + ROWS)
                block = score_ref[there, c : c + ROWS]
                grad = jnp.exp(block - own) + jnp.exp(block - cols_ref[0:1, lanes])
                grad = grad - jnp.where(row_id == ids_ref[0:1, lanes], 1.0, 0.0)
                g_scr[at, lanes] = grad.astype(BF16)
            start += score_ref.shape[1]

    for n in range(0, WIDTH, 256):
        at = slice(n, n + 256)
        partial, start = 0.0, 0
        for ref in cols:
            part = g_scr[:, start : start + ref.shape[0]]
            partial += jnp.dot(part, ref[:, at], preferred_element_type=F32)
            start += ref.shape[0]
        partial = partial * INV_TEMP
        if add_ref is not None:
            partial = partial + add_ref[:, at].astype(F32)
        out_ref[:, at] = partial.astype(out_ref.dtype)


def final_kernel(own, r1, r2, q_ref, p_ref, gq_ref, gp_ref):
    for part, (raw, out_ref) in enumerate(((q_ref, gq_ref), (p_ref, gp_ref))):
        at = slice(part * ROWS, (part + 1) * ROWS)
        grad = own[at, :] + r1[at, :].astype(F32) + r2[at, :].astype(F32)
        values = raw[...].astype(F32)
        scale = lax.rsqrt(jnp.sum(values * values, axis=1, keepdims=True) + EPS)
        inner = jnp.sum(values * grad, axis=1, keepdims=True)
        out_ref[...] = scale * grad - values * (inner * scale * scale * scale)


def body(q_embed, p_embed, positives):
    core = lax.axis_index("grp") % 2
    coord = jnp.stack([*place(core, lax.axis_index("dev")), core]).astype(jnp.int32)
    pos_row = positives.reshape(1, ROWS)
    shape = jax.ShapeDtypeStruct
    packed = shape((SHARD + PAD, WIDTH), BF16)
    stat = shape((16, ROWS), F32)

    own, plain = pl.pallas_call(
        norm_kernel,
        out_shape=[packed, shape((SHARD, WIDTH), BF16)],
        in_specs=[HBM] * 3,
        out_specs=[VMEM] * 2,
        scratch_shapes=[
            pltpu.VMEM((1, ROWS), jnp.int32),
            pltpu.VMEM((2, ROWS, WIDTH), BF16),
            pltpu.SemaphoreType.DMA((3,)),
        ],
        compiler_params=params(60),
        name="unit_rows",
    )(pos_row, q_embed, p_embed)

    def gate(value, *others):
        return pl.pallas_call(
            gate_kernel,
            out_shape=shape(value.shape, value.dtype),
            in_specs=[ANY] * (1 + len(others)),
            out_specs=ANY,
            input_output_aliases={0: 0},
            compiler_params=params(1),
            name="gate",
        )(value, *others)

    far = shift(own, 0, 1, 0)[:SHARD]
    b1, b3 = shift(plain, 1, 0, 0), shift(plain, -1, 0, 0)
    a1, a3 = shift(own, 0, 0, 1), shift(own, 0, 0, -1)
    rows = [own, a1, shift(a1, 0, 0, 1), a3]
    cols = [plain, b1, shift(b3, -1, 0, 0), b3]
    far = gate(far, rows[2], cols[2])
    far_cols = [far] + [shift(far, d, 0, 0) for d in (1, 2, -1)]

    def forward(stage, extra, rows, cols):
        counts = (SHARD,) * len(cols)
        out_shape = [
            shape((NX * SHARD, sum(counts)), F32),
            stat,
            shape((sum(counts), WIDTH), BF16),
        ]
        if stage == 0:
            out_shape += [shape((NX * SHARD, WIDTH), BF16), shape((8, ROWS), jnp.int32)]
        operands = (*extra, *rows, *cols)
        return pl.pallas_call(
            functools.partial(fwd_kernel, stage, counts),
            out_shape=out_shape,
            in_specs=[SMEM] + [VMEM] * len(operands),
            out_specs=[VMEM] * len(out_shape),
            compiler_params=params(20),
            name="scores_" + str(stage),
        )(coord, *operands)

    score0, stat0, col0, *all_rows = forward(0, [], rows, cols)
    score1, stat1, col1 = forward(1, [], all_rows, far_cols[:2])
    score2, stat1, col2 = forward(2, [stat0, stat1, pos_row], all_rows, far_cols[2:])

    stats = [stat1] + [shift(stat1, 0, 0, d) for d in range(1, NX)]
    joined = pl.pallas_call(
        join_kernel,
        out_shape=stat,
        in_specs=[SMEM] + [VMEM] * NX,
        out_specs=VMEM,
        scratch_shapes=[pltpu.VMEM((NX, 8, ROWS), F32), pltpu.VMEM((NX, 8, ROWS), F32)],
        compiler_params=params(2),
        name="join_logs",
    )(coord, *stats)
    pair = jnp.concatenate([joined, shift(joined, 0, 1, 0)], axis=0)
    quads = [pair] + [shift(pair, d, 0, 0) for d in range(1, NY)]
    count = NY * NZ * NX
    lz_rows, lz_cols, ids, loss = pl.pallas_call(
        mid_kernel,
        out_shape=[
            shape((2 * NX, ROWS), F32),
            shape((1, NY * NZ * SHARD), F32),
            shape((1, NY * NZ * SHARD), jnp.int32),
            shape((1, ROWS), F32),
        ],
        in_specs=[SMEM] + [VMEM] * NY,
        out_specs=[VMEM] * 4,
        scratch_shapes=[pltpu.VMEM((count + NY * NZ, 8, ROWS), F32)],
        compiler_params=params(4),
        name="log_totals",
    )(coord, *quads)

    def backward(k, dtype, *extra):
        return pl.pallas_call(
            functools.partial(bwd_kernel, k),
            out_shape=shape((SHARD, WIDTH), dtype),
            in_specs=[VMEM] * (9 + len(extra)),
            out_specs=VMEM,
            scratch_shapes=[
                pltpu.VMEM((SHARD, NY * NZ * SHARD), BF16),
                pltpu.VMEM((SHARD, ROWS), F32),
            ],
            compiler_params=params(20),
            cost_estimate=pl.CostEstimate(
                flops=2 * 1024**3, bytes_accessed=6 * 1024**2, transcendentals=1024**2
            ),
            name="grads_" + str(k),
        )(lz_rows, lz_cols, ids, score0, score1, score2, col0, col1, col2, *extra)

    groups = lax.axis_size("grp")

    def add_over(value, step):
        return value + lax.ppermute(value, "grp", [(g, g ^ step) for g in range(groups)])

    part2 = shift(backward(2, BF16), 0, 0, -2)
    loss = add_over(loss, 1)
    part1 = shift(backward(1, BF16, loss), 0, 0, -1)
    loss = add_over(loss, 2)
    part3 = shift(backward(3, BF16, loss), 0, 0, -3)
    loss = add_over(loss, 4)
    own_part = backward(0, F32, loss, part2)
    mean_loss = loss[0, 0] / (ROWS * groups * lax.axis_size("dev"))
    grad_q, grad_p = pl.pallas_call(
        final_kernel,
        out_shape=[shape((ROWS, WIDTH), F32)] * 2,
        in_specs=[VMEM] * 5,
        out_specs=[VMEM] * 2,
        compiler_params=params(16),
        name="pull_back",
    )(own_part, part1, part3, q_embed, p_embed)
    return (mean_loss, grad_q, grad_p)


def solution(mesh):
    return jax.shard_map(
        body,
        mesh=mesh,
        in_specs=(P(("grp", "dev"), None), P(("grp", "dev"), None), P(("grp", "dev"))),
        out_specs=(P(), P(("grp", "dev"), None), P(("grp", "dev"), None)),
        check_vma=False,
    )
```

```python
import functools

import jax
import jax.numpy as jnp
from jax import lax
from jax.experimental import pallas as pl
from jax.experimental.pallas import tpu as pltpu
from jax.sharding import PartitionSpec as P

INV_TEMP = 100.0
EPS = 1e-06
NY, NZ, NX = 4, 2, 4
ROWS = 128
SHARD = 2 * ROWS
PAD = 16
WIDTH = 1024
STRIP = 32
MASKED = -1e30
F32 = jnp.float32
BF16 = jnp.bfloat16
VMEM = pl.BlockSpec(memory_space=pltpu.VMEM)
ANY = pl.BlockSpec(memory_space=pl.ANY)
HBM = pl.BlockSpec(memory_space=pltpu.HBM)
SMEM = pl.BlockSpec(memory_space=pltpu.SMEM)
NT = (((1,), (1,)), ((), ()))


def dev_index(core, b, z, a):
    y, x = (a, b) if core else (b, a)
    return (y % NY) * (NZ * NX) + (z % NZ) * NX + x % NX


def shift(value, db, dz, da):
    groups, devs = lax.axis_size("grp"), lax.axis_size("dev")
    pairs = [
        (grp * devs + dev_index(grp % 2, b, z, a), grp * devs + dev_index(grp % 2, b + db, z + dz, a + da))
        for grp in range(groups)
        for b in range(NY)
        for z in range(NZ)
        for a in range(NX)
    ]
    return lax.ppermute(value, ("grp", "dev"), pairs)


def place(core, index):
    high, low = index // (NZ * NX), index % NX
    swap = core == 1
    return jnp.where(swap, low, high), (index // NX) % NZ, jnp.where(swap, high, low)


def slot_of(owner, coord):
    high, low = owner >> 3, owner & 3
    swap = coord[3] == 1
    b, a = jnp.where(swap, low, high), jnp.where(swap, high, low)
    return (coord[0] - b) & 3, ((owner >> 2) & 1) ^ coord[1], (coord[2] - a) & 3


def params(mib):
    return pltpu.CompilerParams(vmem_limit_bytes=mib * 1024 * 1024)


def lse2(left, right):
    top = jnp.maximum(left, right)
    return top + jnp.log(jnp.exp(left - top) + jnp.exp(right - top))


def iota(shape, dim):
    return lax.broadcasted_iota(jnp.int32, shape, dim)


def to_row(column):
    eye = iota((ROWS, ROWS), 0) == iota((ROWS, ROWS), 1)
    return jnp.sum(jnp.where(eye, column, 0.0), axis=0, keepdims=True)


def to_column(row):
    eye = iota((ROWS, ROWS), 0) == iota((ROWS, ROWS), 1)
    return jnp.sum(jnp.where(eye, row, 0.0), axis=1, keepdims=True)


def norm_kernel(pos_hbm, q_hbm, p_hbm, out_ref, plain_ref, pos_ref, raw_ref, sems):
    copies = [
        pltpu.make_async_copy(q_hbm, raw_ref.at[0], sems.at[0]),
        pltpu.make_async_copy(p_hbm, raw_ref.at[1], sems.at[1]),
        pltpu.make_async_copy(pos_hbm, pos_ref, sems.at[2]),
    ]
    for copy in copies:
        copy.start()
    for part in range(2):
        copies[part].wait()
        values = raw_ref[part].astype(F32)
        scale = lax.rsqrt(jnp.sum(values * values, axis=1, keepdims=True) + EPS)
        unit = (values * scale).astype(BF16)
        out_ref[part * ROWS : (part + 1) * ROWS, :] = unit
        plain_ref[part * ROWS : (part + 1) * ROWS, :] = unit
    copies[2].wait()
    pos = pos_ref[...]
    high = jnp.broadcast_to((pos >> 6).astype(F32), (PAD, ROWS))
    low = jnp.broadcast_to((pos & 63).astype(F32), (PAD, ROWS))
    out_ref[SHARD:, 0:ROWS] = high.astype(BF16)
    out_ref[SHARD:, ROWS : 2 * ROWS] = low.astype(BF16)
    out_ref[SHARD:, 2 * ROWS :] = jnp.zeros((PAD, WIDTH - 2 * ROWS), BF16)


def gate_kernel(*refs):
    del refs


def fwd_kernel(stage, col_counts, *refs):
    if stage < 2:
        coord, *refs = refs
    else:
        coord, before, between, pos_ref, *refs = refs
    parts = len(col_counts)
    if stage == 0:
        rows, cols = refs[:NX], refs[NX : NX + parts]
        score_ref, stat_ref, col_ref, row_ref, place_ref = refs[NX + parts :]
        for k in range(NX):
            row_ref[k * SHARD : (k + 1) * SHARD, :] = rows[k][0:SHARD, :]
            digits = rows[k][SHARD : SHARD + PAD, 0 : 2 * ROWS].astype(F32)
            place_ref[k : k + 1, :] = (digits[0:1, 0:ROWS] * 64.0 + digits[0:1, ROWS:]).astype(
                jnp.int32
            )
        place_ref[NX:, :] = jnp.zeros((8 - NX, ROWS), jnp.int32)
    else:
        row_ref, place_ref, *cols = refs[: 2 + parts]
        score_ref, stat_ref, col_ref = refs[2 + parts :]
    at = 0
    for ref, count in zip(cols, col_counts):
        col_ref[at : at + count, :] = ref[...]
        at += count
    stat_ref[...] = jnp.zeros_like(stat_ref)
    for k in range(NX):
        chunk = slice(k * SHARD, (k + 1) * SHARD)
        block = INV_TEMP * lax.dot_general(
            row_ref[chunk, :], col_ref[...], NT, preferred_element_type=F32
        )
        score_ref[chunk, :] = block
        if stage == 0 and k == 0:
            diagonal = iota((SHARD, SHARD), 0) == iota((SHARD, SHARD), 1)
            score_ref[chunk, 0:SHARD] = jnp.where(diagonal, MASKED, score_ref[chunk, 0:SHARD])
        for part in range(2):
            first = k * SHARD + part * ROWS
            block = score_ref[first : first + ROWS, :]
            top = jnp.max(block, axis=1, keepdims=True)
            total = jnp.sum(jnp.exp(block - top), axis=1, keepdims=True)
            lead = part * NX + k
            stat_ref[lead : lead + 1, :] = to_row(top + jnp.log(total))

    lead_slot = 2 if stage == 2 else 0
    hits = jnp.zeros((ROWS, ROWS), F32)
    for k in range(NX):
        pos = place_ref[k : k + 1, :]
        db, dz, da = slot_of(pos >> 7, coord)
        here = (dz == (1 if stage else 0)) & (da == 0)
        place_row = jnp.where(here, db * ROWS + (pos & 127), -1)
        col_id = to_column(place_row.astype(F32)).astype(jnp.int32)
        for j in range(parts):
            lead = j * SHARD + ROWS
            block = score_ref[k * SHARD : k * SHARD + ROWS, lead : lead + ROWS]
            hit = (iota((ROWS, ROWS), 1) + (lead_slot + j) * ROWS) == col_id
            hits = hits + jnp.where(hit, block, 0.0)
    stat_ref[8:9, :] = jnp.sum(hits, axis=0, keepdims=True)

    if stage == 2:
        stat_ref[0:8, :] = lse2(lse2(stat_ref[0:8, :], between[0:8, :]), before[0:8, :])
        stat_ref[8:9, :] = stat_ref[8:9, :] + (between[8:9, :] + before[8:9, :])
        stat_ref[9:10, :] = pos_ref[...].astype(F32)


def join_kernel(coord, s0, s1, s2, s3, out_ref, scr, hit_scr):
    a = coord[2]
    stats = (s0, s1, s2, s3)
    for d in range(NX):
        at = (a - d) & 3
        for part in range(2):
            for k in range(NX):
                scr[at, part * NX + k : part * NX + k + 1, :] = stats[d][
                    part * NX + (k - d) % NX : part * NX + (k - d) % NX + 1, :
                ]
        hit_scr[at, 0:1, :] = stats[d][8:9, :]
        out_ref[8 + d : 9 + d, :] = stats[d][9:10, :]
    top = jnp.maximum(jnp.maximum(scr[0], scr[1]), jnp.maximum(scr[2], scr[3]))
    total = jnp.exp(scr[0] - top) + jnp.exp(scr[1] - top)
    total = total + jnp.exp(scr[2] - top) + jnp.exp(scr[3] - top)
    out_ref[0:8, :] = top + jnp.log(total)
    hit = hit_scr[0, 0:1, :] + hit_scr[1, 0:1, :] + hit_scr[2, 0:1, :] + hit_scr[3, 0:1, :]
    out_ref[12:13, :] = hit
    out_ref[13:16, :] = jnp.zeros((3, ROWS), F32)


def mid_kernel(coord, c0, c1, c2, c3, rows_ref, cols_ref, ids_ref, loss_ref, sum_scr):
    parts = (c0, c1, c2, c3)
    count = NY * NZ * NX

    def table(first_row):
        return jnp.concatenate(
            [
                parts[jb][jz * 16 + first_row : jz * 16 + first_row + NX, :]
                for jb in range(NY)
                for jz in range(NZ)
            ],
            axis=0,
        )

    log_b, log_a, pos = table(0), table(4), table(8).astype(jnp.int32)
    lane = pos & 127
    db, dz, da = slot_of(pos >> 7, coord)
    slot = (db * NZ + dz) * NX + da
    log_a_pos = jnp.zeros((count, ROWS), F32)
    for r in range(count):
        picked = jnp.take_along_axis(
            jnp.broadcast_to(log_a[r : r + 1, :], (count, ROWS)), lane, axis=1
        )
        log_a_pos = jnp.where(slot == r, picked, log_a_pos)
    lzq = lse2(log_b, log_a_pos)

    part_high = lzq.astype(BF16).astype(F32)
    part_mid = (lzq - part_high).astype(BF16).astype(F32)
    part_low = lzq - part_high - part_mid
    lane_row = iota((1, ROWS), 1).astype(F32)
    total = jnp.zeros((5 * count, ROWS), F32)
    for group in range(0, count, 2):
        left, right = [], []
        for r in (group, group + 1):
            chosen = iota((count, ROWS), 0) == slot[r : r + 1, :]
            values = (
                part_high[r : r + 1, :],
                part_mid[r : r + 1, :],
                part_low[r : r + 1, :],
                jnp.full((1, ROWS), float(r), F32),
                lane_row,
            )
            left.append(
                jnp.concatenate([jnp.where(chosen, v, 0.0) for v in values], axis=0).astype(BF16)
            )
            right.append((iota((ROWS, ROWS), 0) == lane[r : r + 1, :]).astype(F32).astype(BF16))
        total = total + lax.dot_general(
            jnp.concatenate(left, axis=1),
            jnp.concatenate(right, axis=1),
            NT,
            preferred_element_type=F32,
        )
    lzp = (total[0:count] + total[count : 2 * count]) + total[2 * count : 3 * count]
    from_slot = total[3 * count : 4 * count].astype(jnp.int32)
    from_lane = total[4 * count :].astype(jnp.int32)
    id_q = slot * SHARD + ROWS + lane
    id_p = from_slot * SHARD + from_lane

    rows_ref[0:NX, :] = lzq[0:NX, :]
    rows_ref[NX : 2 * NX, :] = lzp[0:NX, :]
    for jb in range(NY):
        for jz in range(NZ):
            r = (jb * NZ + jz) * NX
            at = (jz * NY + jb) * SHARD
            for part, (lz, ids) in enumerate(((lzq, id_q), (lzp, id_p))):
                here = slice(at + part * ROWS, at + (part + 1) * ROWS)
                cols_ref[0:1, here] = lz[r : r + 1, :]
                ids_ref[0:1, here] = ids[r : r + 1, :]

    for jb in range(NY):
        for jz in range(NZ):
            lead = ((coord[0] - jb) & 3) * NZ + (coord[1] ^ jz)
            for ka in range(NX):
                r = (jb * NZ + jz) * NX + ka
                sum_scr[lead * NX + ((coord[2] - ka) & 3), 0:1, :] = lzq[r : r + 1, :]
            sum_scr[count + lead, 0:1, :] = -parts[jb][jz * 16 + 12 : jz * 16 + 13, :]
    row = sum_scr[0, 0:1, :]
    for r in range(1, count + NY * NZ):
        row = row + sum_scr[r, 0:1, :]
    loss_ref[...] = jnp.broadcast_to(jnp.sum(row, axis=1, keepdims=True), (1, ROWS))


def bwd_kernel(k, rows_ref, cols_ref, ids_ref, *refs):
    scores, cols = refs[0:3], refs[3:6]
    add_ref, out_ref, g_scr, own_scr, sum_scr = (refs[-5] if k == 0 else None), *refs[-4:]
    for part in range(2):
        own = to_column(rows_ref[part * NX + k : part * NX + k + 1, :])
        own_scr[part * ROWS : (part + 1) * ROWS, :] = jnp.broadcast_to(own, (ROWS, ROWS))

    start = 0
    for piece, (score_ref, col_ref) in enumerate(zip(scores, cols)):
        width = score_ref.shape[1]
        for r in range(0, SHARD, STRIP):
            rows = slice(r, r + STRIP)
            own = own_scr[rows, :]
            row_id = iota((STRIP, ROWS), 0) + (k * SHARD + r)
            for c in range(0, width, ROWS):
                lanes = slice(start + c, start + c + ROWS)
                block = score_ref[k * SHARD + r : k * SHARD + r + STRIP, c : c + ROWS]
                grad = jnp.exp(block - own) + jnp.exp(block - cols_ref[0:1, lanes])
                grad = grad - jnp.where(row_id == ids_ref[0:1, lanes], 1.0, 0.0)
                g_scr[rows, lanes] = grad.astype(BF16)
        for n in range(0, WIDTH, 256):
            at = slice(n, n + 256)
            partial = jnp.dot(
                g_scr[:, start : start + width], col_ref[:, at], preferred_element_type=F32
            )
            if piece:
                partial = partial + sum_scr[:, at]
            if piece < len(cols) - 1:
                sum_scr[:, at] = partial
                continue
            partial = partial * INV_TEMP
            if add_ref is not None:
                partial = partial + add_ref[:, at].astype(F32)
            out_ref[:, at] = partial.astype(out_ref.dtype)
        start += width


def final_kernel(own, r1, r2, q_ref, p_ref, gq_ref, gp_ref):
    for part, (raw, out_ref) in enumerate(((q_ref, gq_ref), (p_ref, gp_ref))):
        at = slice(part * ROWS, (part + 1) * ROWS)
        grad = own[at, :] + r1[at, :].astype(F32) + r2[at, :].astype(F32)
        values = raw[...].astype(F32)
        scale = lax.rsqrt(jnp.sum(values * values, axis=1, keepdims=True) + EPS)
        inner = jnp.sum(values * grad, axis=1, keepdims=True)
        out_ref[...] = scale * grad - values * (inner * scale * scale * scale)


def body(q_embed, p_embed, positives):
    core = lax.axis_index("grp") % 2
    coord = jnp.stack([*place(core, lax.axis_index("dev")), core]).astype(jnp.int32)
    pos_row = positives.reshape(1, ROWS)
    shape = jax.ShapeDtypeStruct
    packed = shape((SHARD + PAD, WIDTH), BF16)
    stat = shape((16, ROWS), F32)

    own, plain = pl.pallas_call(
        norm_kernel,
        out_shape=[packed, shape((SHARD, WIDTH), BF16)],
        in_specs=[HBM] * 3,
        out_specs=[VMEM] * 2,
        scratch_shapes=[
            pltpu.VMEM((1, ROWS), jnp.int32),
            pltpu.VMEM((2, ROWS, WIDTH), BF16),
            pltpu.SemaphoreType.DMA((3,)),
        ],
        compiler_params=params(60),
        name="unit_rows",
    )(pos_row, q_embed, p_embed)

    def gate(value, *others):
        return pl.pallas_call(
            gate_kernel,
            out_shape=shape(value.shape, value.dtype),
            in_specs=[ANY] * (1 + len(others)),
            out_specs=ANY,
            input_output_aliases={0: 0},
            compiler_params=params(1),
            name="gate",
        )(value, *others)

    far = shift(own, 0, 1, 0)[:SHARD]
    b1, b3 = shift(plain, 1, 0, 0), shift(plain, -1, 0, 0)
    a1, a3 = shift(own, 0, 0, 1), shift(own, 0, 0, -1)
    rows = [own, a1, shift(a1, 0, 0, 1), a3]
    cols = [plain, b1, shift(b3, -1, 0, 0), b3]
    far = gate(far, cols[2])
    far_cols = [far] + [shift(far, d, 0, 0) for d in (1, 2, -1)]

    def forward(stage, extra, rows, cols):
        counts = (SHARD,) * len(cols)
        out_shape = [
            shape((NX * SHARD, sum(counts)), F32),
            stat,
            shape((sum(counts), WIDTH), BF16),
        ]
        if stage == 0:
            out_shape += [shape((NX * SHARD, WIDTH), BF16), shape((8, ROWS), jnp.int32)]
        operands = (*extra, *rows, *cols)
        return pl.pallas_call(
            functools.partial(fwd_kernel, stage, counts),
            out_shape=out_shape,
            in_specs=[SMEM] + [VMEM] * len(operands),
            out_specs=[VMEM] * len(out_shape),
            compiler_params=params(20),
            name="scores_" + str(stage),
        )(coord, *operands)

    score0, stat0, col0, *all_rows = forward(0, [], rows, cols)
    score1, stat1, col1 = forward(1, [], all_rows, far_cols[:2])
    score2, stat1, col2 = forward(2, [stat0, stat1, pos_row], all_rows, far_cols[2:])

    stats = [stat1] + [shift(stat1, 0, 0, d) for d in range(1, NX)]
    joined = pl.pallas_call(
        join_kernel,
        out_shape=stat,
        in_specs=[SMEM] + [VMEM] * NX,
        out_specs=VMEM,
        scratch_shapes=[pltpu.VMEM((NX, 8, ROWS), F32), pltpu.VMEM((NX, 8, ROWS), F32)],
        compiler_params=params(2),
        name="join_logs",
    )(coord, *stats)
    pair = jnp.concatenate([joined, shift(joined, 0, 1, 0)], axis=0)
    quads = [pair] + [shift(pair, d, 0, 0) for d in range(1, NY)]
    count = NY * NZ * NX
    lz_rows, lz_cols, ids, loss = pl.pallas_call(
        mid_kernel,
        out_shape=[
            shape((2 * NX, ROWS), F32),
            shape((1, NY * NZ * SHARD), F32),
            shape((1, NY * NZ * SHARD), jnp.int32),
            shape((1, ROWS), F32),
        ],
        in_specs=[SMEM] + [VMEM] * NY,
        out_specs=[VMEM] * 4,
        scratch_shapes=[pltpu.VMEM((count + NY * NZ, 8, ROWS), F32)],
        compiler_params=params(4),
        name="log_totals",
    )(coord, *quads)

    def backward(k, dtype, *extra):
        return pl.pallas_call(
            functools.partial(bwd_kernel, k),
            out_shape=shape((SHARD, WIDTH), dtype),
            in_specs=[VMEM] * (9 + len(extra)),
            out_specs=VMEM,
            scratch_shapes=[
                pltpu.VMEM((SHARD, NY * NZ * SHARD), BF16),
                pltpu.VMEM((SHARD, ROWS), F32),
                pltpu.VMEM((SHARD, WIDTH), F32),
            ],
            compiler_params=params(20),
            cost_estimate=pl.CostEstimate(
                flops=2 * 1024**3, bytes_accessed=6 * 1024**2, transcendentals=1024**2
            ),
            name="grads_" + str(k),
        )(lz_rows, lz_cols, ids, score0, score1, score2, col0, col1, col2, *extra)

    groups = lax.axis_size("grp")

    def add_over(value, step):
        return value + lax.ppermute(value, "grp", [(g, g ^ step) for g in range(groups)])

    part2 = shift(backward(2, BF16), 0, 0, -2)
    loss = add_over(loss, 1)
    part1 = shift(backward(1, BF16, loss), 0, 0, -1)
    loss = add_over(loss, 2)
    part3 = shift(backward(3, BF16, loss), 0, 0, -3)
    loss = add_over(loss, 4)
    own_part = backward(0, F32, loss, part2)
    mean_loss = loss[0, 0] / (ROWS * groups * lax.axis_size("dev"))
    grad_q, grad_p = pl.pallas_call(
        final_kernel,
        out_shape=[shape((ROWS, WIDTH), F32)] * 2,
        in_specs=[VMEM] * 5,
        out_specs=[VMEM] * 2,
        compiler_params=params(16),
        name="pull_back",
    )(own_part, part1, part3, q_embed, p_embed)
    return (mean_loss, grad_q, grad_p)


def solution(mesh):
    return jax.shard_map(
        body,
        mesh=mesh,
        in_specs=(P(("grp", "dev"), None), P(("grp", "dev"), None), P(("grp", "dev"))),
        out_specs=(P(), P(("grp", "dev"), None), P(("grp", "dev"), None)),
        check_vma=False,
    )
```

```python
import functools

import jax
import jax.numpy as jnp
from jax import lax
from jax.experimental import pallas as pl
from jax.experimental.pallas import tpu as pltpu
from jax.sharding import PartitionSpec as P

INV_TEMP = 100.0
EPS = 1e-06
NY, NZ, NX = 4, 2, 4
ROWS = 128
SHARD = 2 * ROWS
PAD = 16
WIDTH = 1024
STRIP = 32
MASKED = -1e30
F32 = jnp.float32
BF16 = jnp.bfloat16
VMEM = pl.BlockSpec(memory_space=pltpu.VMEM)
ANY = pl.BlockSpec(memory_space=pl.ANY)
HBM = pl.BlockSpec(memory_space=pltpu.HBM)
SMEM = pl.BlockSpec(memory_space=pltpu.SMEM)
NT = (((1,), (1,)), ((), ()))


def dev_index(core, b, z, a):
    y, x = (a, b) if core else (b, a)
    return (y % NY) * (NZ * NX) + (z % NZ) * NX + x % NX


def shift(value, db, dz, da):
    groups, devs = lax.axis_size("grp"), lax.axis_size("dev")
    pairs = [
        (grp * devs + dev_index(grp % 2, b, z, a), grp * devs + dev_index(grp % 2, b + db, z + dz, a + da))
        for grp in range(groups)
        for b in range(NY)
        for z in range(NZ)
        for a in range(NX)
    ]
    return lax.ppermute(value, ("grp", "dev"), pairs)


def place(core, index):
    high, low = index // (NZ * NX), index % NX
    swap = core == 1
    return jnp.where(swap, low, high), (index // NX) % NZ, jnp.where(swap, high, low)


def slot_of(owner, coord):
    high, low = owner >> 3, owner & 3
    swap = coord[3] == 1
    b, a = jnp.where(swap, low, high), jnp.where(swap, high, low)
    return (coord[0] - b) & 3, ((owner >> 2) & 1) ^ coord[1], (coord[2] - a) & 3


def params(mib):
    return pltpu.CompilerParams(vmem_limit_bytes=mib * 1024 * 1024)


def lse2(left, right):
    top = jnp.maximum(left, right)
    return top + jnp.log(jnp.exp(left - top) + jnp.exp(right - top))


def iota(shape, dim):
    return lax.broadcasted_iota(jnp.int32, shape, dim)


def to_row(column):
    eye = iota((ROWS, ROWS), 0) == iota((ROWS, ROWS), 1)
    return jnp.sum(jnp.where(eye, column, 0.0), axis=0, keepdims=True)


def to_column(row):
    eye = iota((ROWS, ROWS), 0) == iota((ROWS, ROWS), 1)
    return jnp.sum(jnp.where(eye, row, 0.0), axis=1, keepdims=True)


def norm_kernel(pos_hbm, q_hbm, p_hbm, own_hbm, plain_hbm, pos_ref, raw_ref, unit_ref, sems):
    copies = [
        pltpu.make_async_copy(q_hbm, raw_ref.at[0], sems.at[0]),
        pltpu.make_async_copy(p_hbm, raw_ref.at[1], sems.at[1]),
        pltpu.make_async_copy(pos_hbm, pos_ref, sems.at[2]),
    ]
    for copy in copies:
        copy.start()
    sends = []
    for part in range(2):
        copies[part].wait()
        values = raw_ref[part].astype(F32)
        scale = lax.rsqrt(jnp.sum(values * values, axis=1, keepdims=True) + EPS)
        at = pl.ds(part * ROWS, ROWS)
        unit_ref[at, :] = (values * scale).astype(BF16)
        for out, ref in enumerate((own_hbm, plain_hbm)):
            send = pltpu.make_async_copy(
                unit_ref.at[at, :], ref.at[at, :], sems.at[3 + 2 * part + out]
            )
            send.start()
            sends.append(send)
    copies[2].wait()
    pos = pos_ref[...]
    high = jnp.broadcast_to((pos >> 6).astype(F32), (PAD, ROWS))
    low = jnp.broadcast_to((pos & 63).astype(F32), (PAD, ROWS))
    unit_ref[SHARD:, 0:ROWS] = high.astype(BF16)
    unit_ref[SHARD:, ROWS : 2 * ROWS] = low.astype(BF16)
    unit_ref[SHARD:, 2 * ROWS :] = jnp.zeros((PAD, WIDTH - 2 * ROWS), BF16)
    tail = pl.ds(SHARD, PAD)
    send = pltpu.make_async_copy(unit_ref.at[tail, :], own_hbm.at[tail, :], sems.at[7])
    send.start()
    sends.append(send)
    for send in sends:
        send.wait()


def gate_kernel(*refs):
    del refs


def fwd_kernel(stage, col_counts, *refs):
    if stage < 2:
        coord, *refs = refs
    else:
        coord, before, between, pos_ref, *refs = refs
    parts = len(col_counts)
    if stage == 0:
        rows, cols = refs[:NX], refs[NX : NX + parts]
        score_ref, stat_ref, col_ref, row_ref, place_ref = refs[NX + parts :]
        for k in range(NX):
            row_ref[k * SHARD : (k + 1) * SHARD, :] = rows[k][0:SHARD, :]
            digits = rows[k][SHARD : SHARD + PAD, 0 : 2 * ROWS].astype(F32)
            place_ref[k : k + 1, :] = (digits[0:1, 0:ROWS] * 64.0 + digits[0:1, ROWS:]).astype(
                jnp.int32
            )
        place_ref[NX:, :] = jnp.zeros((8 - NX, ROWS), jnp.int32)
    else:
        row_ref, place_ref, *cols = refs[: 2 + parts]
        score_ref, stat_ref, col_ref = refs[2 + parts :]
    at = 0
    for ref, count in zip(cols, col_counts):
        col_ref[at : at + count, :] = ref[...]
        at += count
    stat_ref[...] = jnp.zeros_like(stat_ref)
    for k in range(NX):
        chunk = slice(k * SHARD, (k + 1) * SHARD)
        block = INV_TEMP * lax.dot_general(
            row_ref[chunk, :], col_ref[...], NT, preferred_element_type=F32
        )
        score_ref[chunk, :] = block
        if stage == 0 and k == 0:
            diagonal = iota((SHARD, SHARD), 0) == iota((SHARD, SHARD), 1)
            score_ref[chunk, 0:SHARD] = jnp.where(diagonal, MASKED, score_ref[chunk, 0:SHARD])
        for part in range(2):
            first = k * SHARD + part * ROWS
            block = score_ref[first : first + ROWS, :]
            top = jnp.max(block, axis=1, keepdims=True)
            total = jnp.sum(jnp.exp(block - top), axis=1, keepdims=True)
            lead = part * NX + k
            stat_ref[lead : lead + 1, :] = to_row(top + jnp.log(total))

    lead_slot = 2 if stage == 2 else 0
    hits = jnp.zeros((ROWS, ROWS), F32)
    for k in range(NX):
        pos = place_ref[k : k + 1, :]
        db, dz, da = slot_of(pos >> 7, coord)
        here = (dz == (1 if stage else 0)) & (da == 0)
        place_row = jnp.where(here, db * ROWS + (pos & 127), -1)
        col_id = to_column(place_row.astype(F32)).astype(jnp.int32)
        for j in range(parts):
            lead = j * SHARD + ROWS
            block = score_ref[k * SHARD : k * SHARD + ROWS, lead : lead + ROWS]
            hit = (iota((ROWS, ROWS), 1) + (lead_slot + j) * ROWS) == col_id
            hits = hits + jnp.where(hit, block, 0.0)
    stat_ref[8:9, :] = jnp.sum(hits, axis=0, keepdims=True)

    if stage == 2:
        stat_ref[0:8, :] = lse2(lse2(stat_ref[0:8, :], between[0:8, :]), before[0:8, :])
        stat_ref[8:9, :] = stat_ref[8:9, :] + (between[8:9, :] + before[8:9, :])
        stat_ref[9:10, :] = pos_ref[...].astype(F32)


def join_kernel(coord, s0, s1, s2, s3, out_ref, scr, hit_scr):
    a = coord[2]
    stats = (s0, s1, s2, s3)
    for d in range(NX):
        at = (a - d) & 3
        for part in range(2):
            for k in range(NX):
                scr[at, part * NX + k : part * NX + k + 1, :] = stats[d][
                    part * NX + (k - d) % NX : part * NX + (k - d) % NX + 1, :
                ]
        hit_scr[at, 0:1, :] = stats[d][8:9, :]
        out_ref[8 + d : 9 + d, :] = stats[d][9:10, :]
    top = jnp.maximum(jnp.maximum(scr[0], scr[1]), jnp.maximum(scr[2], scr[3]))
    total = jnp.exp(scr[0] - top) + jnp.exp(scr[1] - top)
    total = total + jnp.exp(scr[2] - top) + jnp.exp(scr[3] - top)
    out_ref[0:8, :] = top + jnp.log(total)
    hit = hit_scr[0, 0:1, :] + hit_scr[1, 0:1, :] + hit_scr[2, 0:1, :] + hit_scr[3, 0:1, :]
    out_ref[12:13, :] = hit
    out_ref[13:16, :] = jnp.zeros((3, ROWS), F32)


def mid_kernel(coord, c0, c1, c2, c3, rows_ref, cols_ref, ids_ref, loss_ref, sum_scr):
    parts = (c0, c1, c2, c3)
    count = NY * NZ * NX

    def table(first_row):
        return jnp.concatenate(
            [
                parts[jb][jz * 16 + first_row : jz * 16 + first_row + NX, :]
                for jb in range(NY)
                for jz in range(NZ)
            ],
            axis=0,
        )

    log_b, log_a, pos = table(0), table(4), table(8).astype(jnp.int32)
    lane = pos & 127
    db, dz, da = slot_of(pos >> 7, coord)
    slot = (db * NZ + dz) * NX + da
    log_a_pos = jnp.zeros((count, ROWS), F32)
    for r in range(count):
        picked = jnp.take_along_axis(
            jnp.broadcast_to(log_a[r : r + 1, :], (count, ROWS)), lane, axis=1
        )
        log_a_pos = jnp.where(slot == r, picked, log_a_pos)
    lzq = lse2(log_b, log_a_pos)

    part_high = lzq.astype(BF16).astype(F32)
    part_mid = (lzq - part_high).astype(BF16).astype(F32)
    part_low = lzq - part_high - part_mid
    lane_row = iota((1, ROWS), 1).astype(F32)
    total = jnp.zeros((5 * count, ROWS), F32)
    for group in range(0, count, 2):
        left, right = [], []
        for r in (group, group + 1):
            chosen = iota((count, ROWS), 0) == slot[r : r + 1, :]
            values = (
                part_high[r : r + 1, :],
                part_mid[r : r + 1, :],
                part_low[r : r + 1, :],
                jnp.full((1, ROWS), float(r), F32),
                lane_row,
            )
            left.append(
                jnp.concatenate([jnp.where(chosen, v, 0.0) for v in values], axis=0).astype(BF16)
            )
            right.append((iota((ROWS, ROWS), 0) == lane[r : r + 1, :]).astype(F32).astype(BF16))
        total = total + lax.dot_general(
            jnp.concatenate(left, axis=1),
            jnp.concatenate(right, axis=1),
            NT,
            preferred_element_type=F32,
        )
    lzp = (total[0:count] + total[count : 2 * count]) + total[2 * count : 3 * count]
    from_slot = total[3 * count : 4 * count].astype(jnp.int32)
    from_lane = total[4 * count :].astype(jnp.int32)
    id_q = slot * SHARD + ROWS + lane
    id_p = from_slot * SHARD + from_lane

    rows_ref[0:NX, :] = lzq[0:NX, :]
    rows_ref[NX : 2 * NX, :] = lzp[0:NX, :]
    for jb in range(NY):
        for jz in range(NZ):
            r = (jb * NZ + jz) * NX
            at = (jz * NY + jb) * SHARD
            for part, (lz, ids) in enumerate(((lzq, id_q), (lzp, id_p))):
                here = slice(at + part * ROWS, at + (part + 1) * ROWS)
                cols_ref[0:1, here] = lz[r : r + 1, :]
                ids_ref[0:1, here] = ids[r : r + 1, :]

    for jb in range(NY):
        for jz in range(NZ):
            lead = ((coord[0] - jb) & 3) * NZ + (coord[1] ^ jz)
            for ka in range(NX):
                r = (jb * NZ + jz) * NX + ka
                sum_scr[lead * NX + ((coord[2] - ka) & 3), 0:1, :] = lzq[r : r + 1, :]
            sum_scr[count + lead, 0:1, :] = -parts[jb][jz * 16 + 12 : jz * 16 + 13, :]
    row = sum_scr[0, 0:1, :]
    for r in range(1, count + NY * NZ):
        row = row + sum_scr[r, 0:1, :]
    loss_ref[...] = jnp.broadcast_to(jnp.sum(row, axis=1, keepdims=True), (1, ROWS))


def bwd_kernel(k, rows_ref, cols_ref, ids_ref, *refs):
    scores, cols = refs[0:3], refs[3:6]
    add_ref, out_ref, g_scr, own_scr, sum_scr = (refs[-5] if k == 0 else None), *refs[-4:]
    for part in range(2):
        own = to_column(rows_ref[part * NX + k : part * NX + k + 1, :])
        own_scr[part * ROWS : (part + 1) * ROWS, :] = jnp.broadcast_to(own, (ROWS, ROWS))

    start = 0
    for piece, (score_ref, col_ref) in enumerate(zip(scores, cols)):
        width = score_ref.shape[1]
        for r in range(0, SHARD, STRIP):
            rows = slice(r, r + STRIP)
            own = own_scr[rows, :]
            row_id = iota((STRIP, ROWS), 0) + (k * SHARD + r)
            for c in range(0, width, ROWS):
                lanes = slice(start + c, start + c + ROWS)
                block = score_ref[k * SHARD + r : k * SHARD + r + STRIP, c : c + ROWS]
                grad = jnp.exp(block - own) + jnp.exp(block - cols_ref[0:1, lanes])
                grad = grad - jnp.where(row_id == ids_ref[0:1, lanes], 1.0, 0.0)
                g_scr[rows, lanes] = grad.astype(BF16)
        for n in range(0, WIDTH, 256):
            at = slice(n, n + 256)
            partial = jnp.dot(
                g_scr[:, start : start + width], col_ref[:, at], preferred_element_type=F32
            )
            if piece:
                partial = partial + sum_scr[:, at]
            if piece < len(cols) - 1:
                sum_scr[:, at] = partial
                continue
            partial = partial * INV_TEMP
            if add_ref is not None:
                partial = partial + add_ref[:, at].astype(F32)
            out_ref[:, at] = partial.astype(out_ref.dtype)
        start += width


def final_kernel(own, r1, r2, q_ref, p_ref, gq_ref, gp_ref):
    for part, (raw, out_ref) in enumerate(((q_ref, gq_ref), (p_ref, gp_ref))):
        at = slice(part * ROWS, (part + 1) * ROWS)
        grad = own[at, :] + r1[at, :].astype(F32) + r2[at, :].astype(F32)
        values = raw[...].astype(F32)
        scale = lax.rsqrt(jnp.sum(values * values, axis=1, keepdims=True) + EPS)
        inner = jnp.sum(values * grad, axis=1, keepdims=True)
        out_ref[...] = scale * grad - values * (inner * scale * scale * scale)


def body(q_embed, p_embed, positives):
    core = lax.axis_index("grp") % 2
    coord = jnp.stack([*place(core, lax.axis_index("dev")), core]).astype(jnp.int32)
    pos_row = positives.reshape(1, ROWS)
    shape = jax.ShapeDtypeStruct
    packed = shape((SHARD + PAD, WIDTH), BF16)
    stat = shape((16, ROWS), F32)

    own, plain = pl.pallas_call(
        norm_kernel,
        out_shape=[packed, shape((SHARD, WIDTH), BF16)],
        in_specs=[HBM] * 3,
        out_specs=[ANY] * 2,
        scratch_shapes=[
            pltpu.VMEM((1, ROWS), jnp.int32),
            pltpu.VMEM((2, ROWS, WIDTH), BF16),
            pltpu.VMEM((SHARD + PAD, WIDTH), BF16),
            pltpu.SemaphoreType.DMA((8,)),
        ],
        compiler_params=params(60),
        name="unit_rows",
    )(pos_row, q_embed, p_embed)

    def gate(value, *others):
        return pl.pallas_call(
            gate_kernel,
            out_shape=shape(value.shape, value.dtype),
            in_specs=[ANY] * (1 + len(others)),
            out_specs=ANY,
            input_output_aliases={0: 0},
            compiler_params=params(1),
            name="gate",
        )(value, *others)

    far = shift(own, 0, 1, 0)[:SHARD]
    b1, b3 = shift(plain, 1, 0, 0), shift(plain, -1, 0, 0)
    a1, a3 = shift(own, 0, 0, 1), shift(own, 0, 0, -1)
    rows = [own, a1, shift(a1, 0, 0, 1), a3]
    cols = [plain, b1, shift(b3, -1, 0, 0), b3]
    far = gate(far, cols[2])
    far_cols = [far] + [shift(far, d, 0, 0) for d in (1, 2, -1)]

    def forward(stage, extra, rows, cols):
        counts = (SHARD,) * len(cols)
        out_shape = [
            shape((NX * SHARD, sum(counts)), F32),
            stat,
            shape((sum(counts), WIDTH), BF16),
        ]
        if stage == 0:
            out_shape += [shape((NX * SHARD, WIDTH), BF16), shape((8, ROWS), jnp.int32)]
        operands = (*extra, *rows, *cols)
        return pl.pallas_call(
            functools.partial(fwd_kernel, stage, counts),
            out_shape=out_shape,
            in_specs=[SMEM] + [VMEM] * len(operands),
            out_specs=[VMEM] * len(out_shape),
            compiler_params=params(20),
            name="scores_" + str(stage),
        )(coord, *operands)

    score0, stat0, col0, *all_rows = forward(0, [], rows, cols)
    score1, stat1, col1 = forward(1, [], all_rows, far_cols[:2])
    score2, stat1, col2 = forward(2, [stat0, stat1, pos_row], all_rows, far_cols[2:])

    stats = [stat1] + [shift(stat1, 0, 0, d) for d in range(1, NX)]
    joined = pl.pallas_call(
        join_kernel,
        out_shape=stat,
        in_specs=[SMEM] + [VMEM] * NX,
        out_specs=VMEM,
        scratch_shapes=[pltpu.VMEM((NX, 8, ROWS), F32), pltpu.VMEM((NX, 8, ROWS), F32)],
        compiler_params=params(2),
        name="join_logs",
    )(coord, *stats)
    pair = jnp.concatenate([joined, shift(joined, 0, 1, 0)], axis=0)
    quads = [pair] + [shift(pair, d, 0, 0) for d in range(1, NY)]
    count = NY * NZ * NX
    lz_rows, lz_cols, ids, loss = pl.pallas_call(
        mid_kernel,
        out_shape=[
            shape((2 * NX, ROWS), F32),
            shape((1, NY * NZ * SHARD), F32),
            shape((1, NY * NZ * SHARD), jnp.int32),
            shape((1, ROWS), F32),
        ],
        in_specs=[SMEM] + [VMEM] * NY,
        out_specs=[VMEM] * 4,
        scratch_shapes=[pltpu.VMEM((count + NY * NZ, 8, ROWS), F32)],
        compiler_params=params(4),
        name="log_totals",
    )(coord, *quads)

    def backward(k, dtype, *extra):
        return pl.pallas_call(
            functools.partial(bwd_kernel, k),
            out_shape=shape((SHARD, WIDTH), dtype),
            in_specs=[VMEM] * (9 + len(extra)),
            out_specs=VMEM,
            scratch_shapes=[
                pltpu.VMEM((SHARD, NY * NZ * SHARD), BF16),
                pltpu.VMEM((SHARD, ROWS), F32),
                pltpu.VMEM((SHARD, WIDTH), F32),
            ],
            compiler_params=params(20),
            cost_estimate=pl.CostEstimate(
                flops=2 * 1024**3, bytes_accessed=6 * 1024**2, transcendentals=1024**2
            ),
            name="grads_" + str(k),
        )(lz_rows, lz_cols, ids, score0, score1, score2, col0, col1, col2, *extra)

    groups = lax.axis_size("grp")

    def add_over(value, step):
        return value + lax.ppermute(value, "grp", [(g, g ^ step) for g in range(groups)])

    part2 = shift(backward(2, BF16), 0, 0, -2)
    loss = add_over(loss, 1)
    part1 = shift(backward(1, BF16, loss), 0, 0, -1)
    part3 = shift(backward(3, BF16, loss), 0, 0, -3)
    loss = add_over(loss, 2)
    own_part = backward(0, F32, part2)
    loss = add_over(gate(loss, own_part), 4)
    mean_loss = loss[0, 0] / (ROWS * groups * lax.axis_size("dev"))
    grad_q, grad_p = pl.pallas_call(
        final_kernel,
        out_shape=[shape((ROWS, WIDTH), F32)] * 2,
        in_specs=[VMEM] * 5,
        out_specs=[VMEM] * 2,
        compiler_params=params(16),
        name="pull_back",
    )(own_part, part1, part3, q_embed, p_embed)
    return (mean_loss, grad_q, grad_p)


def solution(mesh):
    return jax.shard_map(
        body,
        mesh=mesh,
        in_specs=(P(("grp", "dev"), None), P(("grp", "dev"), None), P(("grp", "dev"))),
        out_specs=(P(), P(("grp", "dev"), None), P(("grp", "dev"), None)),
        check_vma=False,
    )
```

```python
import functools

import jax
import jax.numpy as jnp
from jax import lax
from jax.experimental import pallas as pl
from jax.experimental.pallas import tpu as pltpu
from jax.sharding import PartitionSpec as P

INV_TEMP = 100.0
EPS = 1e-06
NY, NZ, NX = 4, 2, 4
ROWS = 128
SHARD = 2 * ROWS
PAD = 16
WIDTH = 1024
STRIP = 32
MASKED = -1e30
F32 = jnp.float32
BF16 = jnp.bfloat16
VMEM = pl.BlockSpec(memory_space=pltpu.VMEM)
ANY = pl.BlockSpec(memory_space=pl.ANY)
HBM = pl.BlockSpec(memory_space=pltpu.HBM)
SMEM = pl.BlockSpec(memory_space=pltpu.SMEM)
NT = (((1,), (1,)), ((), ()))


def dev_index(core, b, z, a):
    y, x = (a, b) if core else (b, a)
    return (y % NY) * (NZ * NX) + (z % NZ) * NX + x % NX


def shift(value, db, dz, da):
    groups, devs = lax.axis_size("grp"), lax.axis_size("dev")
    pairs = [
        (grp * devs + dev_index(grp % 2, b, z, a), grp * devs + dev_index(grp % 2, b + db, z + dz, a + da))
        for grp in range(groups)
        for b in range(NY)
        for z in range(NZ)
        for a in range(NX)
    ]
    return lax.ppermute(value, ("grp", "dev"), pairs)


def place(core, index):
    high, low = index // (NZ * NX), index % NX
    swap = core == 1
    return jnp.where(swap, low, high), (index // NX) % NZ, jnp.where(swap, high, low)


def slot_of(owner, coord):
    high, low = owner >> 3, owner & 3
    swap = coord[3] == 1
    b, a = jnp.where(swap, low, high), jnp.where(swap, high, low)
    return (coord[0] - b) & 3, ((owner >> 2) & 1) ^ coord[1], (coord[2] - a) & 3


def params(mib):
    return pltpu.CompilerParams(vmem_limit_bytes=mib * 1024 * 1024)


def lse2(left, right):
    top = jnp.maximum(left, right)
    return top + jnp.log(jnp.exp(left - top) + jnp.exp(right - top))


def iota(shape, dim):
    return lax.broadcasted_iota(jnp.int32, shape, dim)


def to_row(column):
    eye = iota((ROWS, ROWS), 0) == iota((ROWS, ROWS), 1)
    return jnp.sum(jnp.where(eye, column, 0.0), axis=0, keepdims=True)


def to_column(row):
    eye = iota((ROWS, ROWS), 0) == iota((ROWS, ROWS), 1)
    return jnp.sum(jnp.where(eye, row, 0.0), axis=1, keepdims=True)


def norm_kernel(pos_hbm, q_hbm, p_hbm, own_hbm, plain_hbm, pos_ref, raw_ref, unit_ref, sems):
    copies = [
        pltpu.make_async_copy(q_hbm, raw_ref.at[0], sems.at[0]),
        pltpu.make_async_copy(p_hbm, raw_ref.at[1], sems.at[1]),
        pltpu.make_async_copy(pos_hbm, pos_ref, sems.at[2]),
    ]
    for copy in copies:
        copy.start()
    sends = []
    for part in range(2):
        copies[part].wait()
        values = raw_ref[part].astype(F32)
        scale = lax.rsqrt(jnp.sum(values * values, axis=1, keepdims=True) + EPS)
        at = pl.ds(part * ROWS, ROWS)
        unit_ref[at, :] = (values * scale).astype(BF16)
        for out, ref in enumerate((own_hbm, plain_hbm)):
            send = pltpu.make_async_copy(
                unit_ref.at[at, :], ref.at[at, :], sems.at[3 + 2 * part + out]
            )
            send.start()
            sends.append(send)
    copies[2].wait()
    pos = pos_ref[...]
    high = jnp.broadcast_to((pos >> 6).astype(F32), (PAD, ROWS))
    low = jnp.broadcast_to((pos & 63).astype(F32), (PAD, ROWS))
    unit_ref[SHARD:, 0:ROWS] = high.astype(BF16)
    unit_ref[SHARD:, ROWS : 2 * ROWS] = low.astype(BF16)
    unit_ref[SHARD:, 2 * ROWS :] = jnp.zeros((PAD, WIDTH - 2 * ROWS), BF16)
    tail = pl.ds(SHARD, PAD)
    send = pltpu.make_async_copy(unit_ref.at[tail, :], own_hbm.at[tail, :], sems.at[7])
    send.start()
    sends.append(send)
    for send in sends:
        send.wait()


def gate_kernel(*refs):
    del refs


def fwd_kernel(stage, col_counts, *refs):
    if stage < 2:
        coord, *refs = refs
    else:
        coord, before, between, pos_ref, *refs = refs
    parts = len(col_counts)
    if stage == 0:
        rows, cols = refs[:NX], refs[NX : NX + parts]
        score_ref, stat_ref, col_ref, row_ref, place_ref = refs[NX + parts :]
        for k in range(NX):
            row_ref[k * SHARD : (k + 1) * SHARD, :] = rows[k][0:SHARD, :]
            digits = rows[k][SHARD : SHARD + PAD, 0 : 2 * ROWS].astype(F32)
            place_ref[k : k + 1, :] = (digits[0:1, 0:ROWS] * 64.0 + digits[0:1, ROWS:]).astype(
                jnp.int32
            )
        place_ref[NX:, :] = jnp.zeros((8 - NX, ROWS), jnp.int32)
    else:
        row_ref, place_ref, *cols = refs[: 2 + parts]
        score_ref, stat_ref, col_ref = refs[2 + parts :]
    at = 0
    for ref, count in zip(cols, col_counts):
        col_ref[at : at + count, :] = ref[...]
        at += count
    stat_ref[...] = jnp.zeros_like(stat_ref)
    for k in range(NX):
        chunk = slice(k * SHARD, (k + 1) * SHARD)
        block = INV_TEMP * lax.dot_general(
            row_ref[chunk, :], col_ref[...], NT, preferred_element_type=F32
        )
        score_ref[chunk, :] = block
        if stage == 0 and k == 0:
            diagonal = iota((SHARD, SHARD), 0) == iota((SHARD, SHARD), 1)
            score_ref[chunk, 0:SHARD] = jnp.where(diagonal, MASKED, score_ref[chunk, 0:SHARD])
        for part in range(2):
            first = k * SHARD + part * ROWS
            block = score_ref[first : first + ROWS, :]
            top = jnp.max(block, axis=1, keepdims=True)
            total = jnp.sum(jnp.exp(block - top), axis=1, keepdims=True)
            lead = part * NX + k
            stat_ref[lead : lead + 1, :] = to_row(top + jnp.log(total))

    lead_slot = 2 if stage == 2 else 0
    hits = jnp.zeros((ROWS, ROWS), F32)
    for k in range(NX):
        pos = place_ref[k : k + 1, :]
        db, dz, da = slot_of(pos >> 7, coord)
        here = (dz == (1 if stage else 0)) & (da == 0)
        place_row = jnp.where(here, db * ROWS + (pos & 127), -1)
        col_id = to_column(place_row.astype(F32)).astype(jnp.int32)
        for j in range(parts):
            lead = j * SHARD + ROWS
            block = score_ref[k * SHARD : k * SHARD + ROWS, lead : lead + ROWS]
            hit = (iota((ROWS, ROWS), 1) + (lead_slot + j) * ROWS) == col_id
            hits = hits + jnp.where(hit, block, 0.0)
    stat_ref[8:9, :] = jnp.sum(hits, axis=0, keepdims=True)

    if stage == 2:
        stat_ref[0:8, :] = lse2(lse2(stat_ref[0:8, :], between[0:8, :]), before[0:8, :])
        stat_ref[8:9, :] = stat_ref[8:9, :] + (between[8:9, :] + before[8:9, :])
        stat_ref[9:10, :] = pos_ref[...].astype(F32)


def join_kernel(coord, s0, s1, s2, s3, out_ref, scr, hit_scr):
    a = coord[2]
    stats = (s0, s1, s2, s3)
    for d in range(NX):
        at = (a - d) & 3
        for part in range(2):
            for k in range(NX):
                scr[at, part * NX + k : part * NX + k + 1, :] = stats[d][
                    part * NX + (k - d) % NX : part * NX + (k - d) % NX + 1, :
                ]
        hit_scr[at, 0:1, :] = stats[d][8:9, :]
        out_ref[8 + d : 9 + d, :] = stats[d][9:10, :]
    top = jnp.maximum(jnp.maximum(scr[0], scr[1]), jnp.maximum(scr[2], scr[3]))
    total = jnp.exp(scr[0] - top) + jnp.exp(scr[1] - top)
    total = total + jnp.exp(scr[2] - top) + jnp.exp(scr[3] - top)
    out_ref[0:8, :] = top + jnp.log(total)
    hit = hit_scr[0, 0:1, :] + hit_scr[1, 0:1, :] + hit_scr[2, 0:1, :] + hit_scr[3, 0:1, :]
    out_ref[12:13, :] = hit
    out_ref[13:16, :] = jnp.zeros((3, ROWS), F32)


def mid_kernel(coord, c0, c1, c2, c3, rows_ref, cols_ref, ids_ref, loss_ref, sum_scr):
    parts = (c0, c1, c2, c3)
    count = NY * NZ * NX

    def table(first_row):
        return jnp.concatenate(
            [
                parts[jb][jz * 16 + first_row : jz * 16 + first_row + NX, :]
                for jb in range(NY)
                for jz in range(NZ)
            ],
            axis=0,
        )

    log_b, log_a, pos = table(0), table(4), table(8).astype(jnp.int32)
    lane = pos & 127
    db, dz, da = slot_of(pos >> 7, coord)
    slot = (db * NZ + dz) * NX + da
    log_a_pos = jnp.zeros((count, ROWS), F32)
    for r in range(count):
        picked = jnp.take_along_axis(
            jnp.broadcast_to(log_a[r : r + 1, :], (count, ROWS)), lane, axis=1
        )
        log_a_pos = jnp.where(slot == r, picked, log_a_pos)
    lzq = lse2(log_b, log_a_pos)

    part_high = lzq.astype(BF16).astype(F32)
    part_mid = (lzq - part_high).astype(BF16).astype(F32)
    part_low = lzq - part_high - part_mid
    lane_row = iota((1, ROWS), 1).astype(F32)
    total = jnp.zeros((5 * count, ROWS), F32)
    for group in range(0, count, 2):
        left, right = [], []
        for r in (group, group + 1):
            chosen = iota((count, ROWS), 0) == slot[r : r + 1, :]
            values = (
                part_high[r : r + 1, :],
                part_mid[r : r + 1, :],
                part_low[r : r + 1, :],
                jnp.full((1, ROWS), float(r), F32),
                lane_row,
            )
            left.append(
                jnp.concatenate([jnp.where(chosen, v, 0.0) for v in values], axis=0).astype(BF16)
            )
            right.append((iota((ROWS, ROWS), 0) == lane[r : r + 1, :]).astype(F32).astype(BF16))
        total = total + lax.dot_general(
            jnp.concatenate(left, axis=1),
            jnp.concatenate(right, axis=1),
            NT,
            preferred_element_type=F32,
        )
    lzp = (total[0:count] + total[count : 2 * count]) + total[2 * count : 3 * count]
    from_slot = total[3 * count : 4 * count].astype(jnp.int32)
    from_lane = total[4 * count :].astype(jnp.int32)
    id_q = slot * SHARD + ROWS + lane
    id_p = from_slot * SHARD + from_lane

    rows_ref[0:NX, :] = lzq[0:NX, :]
    rows_ref[NX : 2 * NX, :] = lzp[0:NX, :]
    for jb in range(NY):
        for jz in range(NZ):
            r = (jb * NZ + jz) * NX
            at = (jz * NY + jb) * SHARD
            for part, (lz, ids) in enumerate(((lzq, id_q), (lzp, id_p))):
                here = slice(at + part * ROWS, at + (part + 1) * ROWS)
                cols_ref[0:1, here] = lz[r : r + 1, :]
                ids_ref[0:1, here] = ids[r : r + 1, :]

    for jb in range(NY):
        for jz in range(NZ):
            lead = ((coord[0] - jb) & 3) * NZ + (coord[1] ^ jz)
            for ka in range(NX):
                r = (jb * NZ + jz) * NX + ka
                sum_scr[lead * NX + ((coord[2] - ka) & 3), 0:1, :] = lzq[r : r + 1, :]
            sum_scr[count + lead, 0:1, :] = -parts[jb][jz * 16 + 12 : jz * 16 + 13, :]
    row = sum_scr[0, 0:1, :]
    for r in range(1, count + NY * NZ):
        row = row + sum_scr[r, 0:1, :]
    loss_ref[...] = jnp.broadcast_to(jnp.sum(row, axis=1, keepdims=True), (1, ROWS))


def bwd_kernel(k, rows_ref, cols_ref, ids_ref, *refs):
    scores, cols = refs[0:3], refs[3:6]
    add_ref, out_ref, g_scr, own_scr, sum_scr = (refs[-5] if k == 0 else None), *refs[-4:]
    for part in range(2):
        own = to_column(rows_ref[part * NX + k : part * NX + k + 1, :])
        own_scr[part * ROWS : (part + 1) * ROWS, :] = jnp.broadcast_to(own, (ROWS, ROWS))

    start = 0
    for piece, (score_ref, col_ref) in enumerate(zip(scores, cols)):
        width = score_ref.shape[1]
        for r in range(0, SHARD, STRIP):
            rows = slice(r, r + STRIP)
            own = own_scr[rows, :]
            row_id = iota((STRIP, ROWS), 0) + (k * SHARD + r)
            for c in range(0, width, ROWS):
                lanes = slice(start + c, start + c + ROWS)
                block = score_ref[k * SHARD + r : k * SHARD + r + STRIP, c : c + ROWS]
                grad = jnp.exp(block - own) + jnp.exp(block - cols_ref[0:1, lanes])
                grad = grad - jnp.where(row_id == ids_ref[0:1, lanes], 1.0, 0.0)
                g_scr[rows, lanes] = grad.astype(BF16)
        for n in range(0, WIDTH, 256):
            at = slice(n, n + 256)
            partial = jnp.dot(
                g_scr[:, start : start + width], col_ref[:, at], preferred_element_type=F32
            )
            if piece:
                partial = partial + sum_scr[:, at]
            if piece < len(cols) - 1:
                sum_scr[:, at] = partial
                continue
            partial = partial * INV_TEMP
            if add_ref is not None:
                partial = partial + add_ref[:, at].astype(F32)
            out_ref[:, at] = partial.astype(out_ref.dtype)
        start += width


def final_kernel(own, r1, r2, q_ref, p_ref, gq_hbm, gp_hbm, out_scr, sems):
    sends = []
    for part, (raw, out_hbm) in enumerate(((q_ref, gq_hbm), (p_ref, gp_hbm))):
        at = slice(part * ROWS, (part + 1) * ROWS)
        grad = own[at, :] + r1[at, :].astype(F32) + r2[at, :].astype(F32)
        values = raw[...].astype(F32)
        scale = lax.rsqrt(jnp.sum(values * values, axis=1, keepdims=True) + EPS)
        inner = jnp.sum(values * grad, axis=1, keepdims=True)
        out_scr[part] = scale * grad - values * (inner * scale * scale * scale)
        send = pltpu.make_async_copy(out_scr.at[part], out_hbm, sems.at[part])
        send.start()
        sends.append(send)
    for send in sends:
        send.wait()


def body(q_embed, p_embed, positives):
    core = lax.axis_index("grp") % 2
    coord = jnp.stack([*place(core, lax.axis_index("dev")), core]).astype(jnp.int32)
    pos_row = positives.reshape(1, ROWS)
    shape = jax.ShapeDtypeStruct
    packed = shape((SHARD + PAD, WIDTH), BF16)
    stat = shape((16, ROWS), F32)

    own, plain = pl.pallas_call(
        norm_kernel,
        out_shape=[packed, shape((SHARD, WIDTH), BF16)],
        in_specs=[HBM] * 3,
        out_specs=[ANY] * 2,
        scratch_shapes=[
            pltpu.VMEM((1, ROWS), jnp.int32),
            pltpu.VMEM((2, ROWS, WIDTH), BF16),
            pltpu.VMEM((SHARD + PAD, WIDTH), BF16),
            pltpu.SemaphoreType.DMA((8,)),
        ],
        compiler_params=params(60),
        name="unit_rows",
    )(pos_row, q_embed, p_embed)

    def gate(value, *others):
        return pl.pallas_call(
            gate_kernel,
            out_shape=shape(value.shape, value.dtype),
            in_specs=[ANY] * (1 + len(others)),
            out_specs=ANY,
            input_output_aliases={0: 0},
            compiler_params=params(1),
            name="gate",
        )(value, *others)

    far = shift(own, 0, 1, 0)[:SHARD]
    b1, b3 = shift(plain, 1, 0, 0), shift(plain, -1, 0, 0)
    a1, a3 = shift(own, 0, 0, 1), shift(own, 0, 0, -1)
    rows = [own, a1, shift(a1, 0, 0, 1), a3]
    cols = [plain, b1, shift(b3, -1, 0, 0), b3]
    far = gate(far, cols[2])
    far_cols = [far] + [shift(far, d, 0, 0) for d in (1, 2, -1)]

    def forward(stage, extra, rows, cols):
        counts = (SHARD,) * len(cols)
        out_shape = [
            shape((NX * SHARD, sum(counts)), F32),
            stat,
            shape((sum(counts), WIDTH), BF16),
        ]
        if stage == 0:
            out_shape += [shape((NX * SHARD, WIDTH), BF16), shape((8, ROWS), jnp.int32)]
        operands = (*extra, *rows, *cols)
        return pl.pallas_call(
            functools.partial(fwd_kernel, stage, counts),
            out_shape=out_shape,
            in_specs=[SMEM] + [VMEM] * len(operands),
            out_specs=[VMEM] * len(out_shape),
            compiler_params=params(20),
            name="scores_" + str(stage),
        )(coord, *operands)

    score0, stat0, col0, *all_rows = forward(0, [], rows, cols)
    score1, stat1, col1 = forward(1, [], all_rows, far_cols[:2])
    score2, stat1, col2 = forward(2, [stat0, stat1, pos_row], all_rows, far_cols[2:])

    stats = [stat1] + [shift(stat1, 0, 0, d) for d in range(1, NX)]
    joined = pl.pallas_call(
        join_kernel,
        out_shape=stat,
        in_specs=[SMEM] + [VMEM] * NX,
        out_specs=VMEM,
        scratch_shapes=[pltpu.VMEM((NX, 8, ROWS), F32), pltpu.VMEM((NX, 8, ROWS), F32)],
        compiler_params=params(2),
        name="join_logs",
    )(coord, *stats)
    pair = jnp.concatenate([joined, shift(joined, 0, 1, 0)], axis=0)
    quads = [pair] + [shift(pair, d, 0, 0) for d in range(1, NY)]
    count = NY * NZ * NX
    lz_rows, lz_cols, ids, loss = pl.pallas_call(
        mid_kernel,
        out_shape=[
            shape((2 * NX, ROWS), F32),
            shape((1, NY * NZ * SHARD), F32),
            shape((1, NY * NZ * SHARD), jnp.int32),
            shape((1, ROWS), F32),
        ],
        in_specs=[SMEM] + [VMEM] * NY,
        out_specs=[VMEM] * 4,
        scratch_shapes=[pltpu.VMEM((count + NY * NZ, 8, ROWS), F32)],
        compiler_params=params(4),
        name="log_totals",
    )(coord, *quads)

    def backward(k, dtype, *extra):
        return pl.pallas_call(
            functools.partial(bwd_kernel, k),
            out_shape=shape((SHARD, WIDTH), dtype),
            in_specs=[VMEM] * (9 + len(extra)),
            out_specs=VMEM,
            scratch_shapes=[
                pltpu.VMEM((SHARD, NY * NZ * SHARD), BF16),
                pltpu.VMEM((SHARD, ROWS), F32),
                pltpu.VMEM((SHARD, WIDTH), F32),
            ],
            compiler_params=params(20),
            cost_estimate=pl.CostEstimate(
                flops=2 * 1024**3, bytes_accessed=6 * 1024**2, transcendentals=1024**2
            ),
            name="grads_" + str(k),
        )(lz_rows, lz_cols, ids, score0, score1, score2, col0, col1, col2, *extra)

    groups = lax.axis_size("grp")

    def add_over(value, step):
        return value + lax.ppermute(value, "grp", [(g, g ^ step) for g in range(groups)])

    part2 = shift(backward(2, BF16), 0, 0, -2)
    loss = add_over(loss, 1)
    part1 = shift(backward(1, BF16, loss), 0, 0, -1)
    part3 = shift(backward(3, BF16, loss), 0, 0, -3)
    loss = add_over(loss, 2)
    own_part = backward(0, F32, part2)
    loss = add_over(gate(loss, own_part), 4)
    mean_loss = loss[0, 0] / (ROWS * groups * lax.axis_size("dev"))
    grad_q, grad_p = pl.pallas_call(
        final_kernel,
        out_shape=[shape((ROWS, WIDTH), F32)] * 2,
        in_specs=[VMEM] * 5,
        out_specs=[ANY] * 2,
        scratch_shapes=[pltpu.VMEM((2, ROWS, WIDTH), F32), pltpu.SemaphoreType.DMA((2,))],
        compiler_params=params(16),
        name="pull_back",
    )(own_part, part1, part3, q_embed, p_embed)
    return (mean_loss, grad_q, grad_p)


def solution(mesh):
    return jax.shard_map(
        body,
        mesh=mesh,
        in_specs=(P(("grp", "dev"), None), P(("grp", "dev"), None), P(("grp", "dev"))),
        out_specs=(P(), P(("grp", "dev"), None), P(("grp", "dev"), None)),
        check_vma=False,
    )
```
